512 devices in a mesh: depth: 4 (over z_lo), row: 8 (over z_hi, core), col: 16 (over x, y).
Axes of the slice: x: 4, y: 4, z: 16 (z_hi: 4, z_lo: 4; z = z_hi * 4 + z_lo), core: 2. Of those that a mesh axis runs over, the one named last changes fastest.
Arguments:
- pair: bfloat16 [384, 384, 128], P('row', 'col'), may hold values from -6 to 6
- cotangent: bfloat16 [384, 384, 128], P('row', 'col'), may hold values from -6 to 6
- w_in: bfloat16 [128, 512], replicated, may hold values from -0.5 to 0.5
- w_gate: bfloat16 [128, 128], replicated, may hold values from -0.5 to 0.5
- w_out: bfloat16 [128, 128], replicated, may hold values from -0.5 to 0.5
- residue_mask: int32 [384], replicated, may hold values 0 or 1
Outputs:
- update: bfloat16 [384, 384, 128], P('row', 'col')
- pair_grad: bfloat16 [384, 384, 128], P('row', 'col')
The draws below stay inside these ranges and needn't reach their ends.
All inputs are finite; a program needn't handle non-finite values.
Results may differ from the reference program's by a relative error of at most 0.024.
Values may be sent and summed in bfloat16 or wider, within the bound.
A program may use at most 64 MiB of HBM per device.

```python
import jax
import jax.numpy as jnp
from jax import lax

N = 384
C = 128
H = 128
N_ROW = 8
N_COL = 16


def touch_ends(values, key, smallest, largest):
    index_at = [jax.random.randint(jax.random.fold_in(key, axis), (), 0, length) for axis, length in enumerate(values.shape)]
    longest = values.shape.index(max(values.shape))
    beside = index_at[:longest] + [(index_at[longest] + 1) % values.shape[longest]] + index_at[longest + 1:]
    return values.at[tuple(index_at)].set(smallest).at[tuple(beside)].set(largest)


def shard_levels(key, dims, pieces, low, high):
    level = 1.0
    for position, parts in pieces:
        steps = jax.random.uniform(jax.random.fold_in(jax.random.fold_in(key, 6), position), (parts,), jnp.float32, low / len(pieces), high / len(pieces))
        level = level * jnp.repeat(jnp.exp(steps), dims[position] // parts).reshape((-1,) + (1,) * (len(dims) - 1 - position))
    return level


def gaussian(rng, shape, spread, most, shards=(), kind=jnp.bfloat16):
    values = spread * jax.random.normal(rng, shape, jnp.float32)
    if shards:
        values = values * shard_levels(rng, shape, shards, -0.22, 0.18)
    return jnp.clip(values, -most, most).astype(kind)


def setup_inputs(seed: int = 0) -> dict:
    keys = jax.random.split(jax.random.key(seed), 7)
    pair = gaussian(keys[0], (N, N, C), 1.0, 6.0, ((0, 8), (1, 16)))
    cotangent = gaussian(keys[1], (N, N, C), 1.0, 6.0, ((0, 8), (1, 16)))
    w_in = gaussian(keys[2], (C, 4 * H), C ** -0.5, 0.5)
    w_gate = gaussian(keys[3], (C, C), C ** -0.5, 0.5)
    w_out = gaussian(keys[4], (H, C), H ** -0.5, 0.5)
    residue_mask = touch_ends((jax.random.randint(keys[5], (N,), 0, 8) < 7).astype(jnp.int32), jax.random.fold_in(keys[5], 1), 0, 1)
    return {"pair": pair, "cotangent": cotangent, "w_in": w_in, "w_gate": w_gate, "w_out": w_out, "residue_mask": residue_mask}


def layer_norm(values):
    average = lax.optimization_barrier(jnp.mean(values, axis=-1, keepdims=True))
    centered = values - average
    variance = lax.optimization_barrier(jnp.mean(centered * centered, axis=-1, keepdims=True))
    inv_std = lax.rsqrt(variance + 1e-05)
    return (centered * inv_std, inv_std)

def norm_back(x_hat, inv_std, upstream):
    first = lax.optimization_barrier(jnp.mean(upstream, axis=-1, keepdims=True))
    second = lax.optimization_barrier(jnp.mean(upstream * x_hat, axis=-1, keepdims=True))
    return inv_std * (upstream - first - x_hat * second)

def flat_dot(left, right):
    shape = left.shape
    result = jnp.dot(left.reshape(-1, shape[-1]), right, preferred_element_type=jnp.float32)
    return result.reshape(shape[:-1] + (right.shape[-1],))

def reference(pair, cotangent, w_in, w_gate, w_out, residue_mask):
    pair_float = pair.astype(jnp.float32)
    x_hat, inv_std = layer_norm(pair_float)
    normed = x_hat.astype(jnp.bfloat16)
    projected = flat_dot(normed, w_in)
    mask_float = residue_mask.astype(jnp.float32)
    pair_mask = (mask_float[:, None] * mask_float[None, :])[..., None]
    sig_a = jax.nn.sigmoid(projected[..., :H])
    val_a = projected[..., H:2 * H]
    sig_b = jax.nn.sigmoid(projected[..., 2 * H:3 * H])
    val_b = projected[..., 3 * H:]
    a_out = (pair_mask * sig_a * val_a).astype(jnp.bfloat16)
    b_out = (pair_mask * sig_b * val_b).astype(jnp.bfloat16)
    a_float = a_out.astype(jnp.float32)
    b_float = b_out.astype(jnp.float32)
    tri_sum = jnp.einsum('ikh,jkh->ijh', a_float, b_float)
    y_hat, tri_std = layer_norm(tri_sum)
    y_norm = y_hat.astype(jnp.bfloat16)
    gate_val = jax.nn.sigmoid(flat_dot(normed, w_gate))
    out_proj = flat_dot(y_norm, w_out)
    update = (gate_val * out_proj).astype(jnp.bfloat16)
    cot_float = cotangent.astype(jnp.float32)
    d_o = (cot_float * gate_val).astype(jnp.bfloat16)
    d_gate_pre = (cot_float * out_proj * gate_val * (1.0 - gate_val)).astype(jnp.bfloat16)
    d_y = flat_dot(d_o, w_out.T)
    tri_grad = norm_back(y_hat, tri_std, d_y).astype(jnp.bfloat16)
    grad_float = tri_grad.astype(jnp.float32)
    width = N // N_COL
    grad_a = jnp.zeros((N, N, H), jnp.float32)
    for block in range(N_COL):
        partial_value = jnp.einsum('ijh,jkh->ikh', grad_float[:, block * width:(block + 1) * width], b_float[block * width:(block + 1) * width])
        rounded = lax.optimization_barrier(partial_value.astype(jnp.bfloat16))
        grad_a = grad_a + rounded.astype(jnp.float32)
    height = N // N_ROW
    grad_b = jnp.zeros((N, N, H), jnp.float32)
    for block in range(N_ROW):
        partial_value = jnp.einsum('ijh,ikh->jkh', grad_float[block * height:(block + 1) * height], a_float[block * height:(block + 1) * height])
        rounded = lax.optimization_barrier(partial_value.astype(jnp.bfloat16))
        grad_b = grad_b + rounded.astype(jnp.float32)
    d_projected = jnp.concatenate([grad_a * pair_mask * val_a * sig_a * (1.0 - sig_a), grad_a * pair_mask * sig_a, grad_b * pair_mask * val_b * sig_b * (1.0 - sig_b), grad_b * pair_mask * sig_b], axis=-1).astype(jnp.bfloat16)
    d_normed = flat_dot(d_projected, w_in.T) + flat_dot(d_gate_pre, w_gate.T)
    pair_grad = norm_back(x_hat, inv_std, d_normed).astype(jnp.bfloat16)
    return (update, pair_grad)
```

```python
import functools

import jax
import jax.numpy as jnp
from jax import lax
from jax.experimental import pallas as pl
from jax.experimental.pallas import tpu as pltpu
from jax.sharding import PartitionSpec as P

MESH = pl.DeviceIdType.MESH
F32 = jnp.float32
BF16 = jnp.bfloat16
SLOT = 32
LANE = 128
PER = LANE // SLOT


def dot(left, right):
    return jnp.dot(left, right, preferred_element_type=F32)


def norm_rows(values):
    average = jnp.mean(values, axis=0, keepdims=True)
    centered = values - average
    variance = jnp.mean(centered * centered, axis=0, keepdims=True)
    inv_std = lax.rsqrt(variance + 1e-05)
    return (centered * inv_std, inv_std)


def norm_back(x_hat, inv_std, upstream):
    first = jnp.mean(upstream, axis=0, keepdims=True)
    second = jnp.mean(upstream * x_hat, axis=0, keepdims=True)
    return inv_std * (upstream - first - x_hat * second)


def lanes(x, v):
    return x[..., v * LANE : (v + 1) * LANE]


def to_matrix(tiles, slot):
    out = []
    for x in tiles:
        groups, rows = x.shape[0] // PER, x.shape[1]
        x = x.reshape(groups, PER, rows, LANE)
        for s in range(PER):
            acc = None
            for c in range(PER):
                y = x[:, c]
                if c != s:
                    y = pltpu.roll(y, (SLOT * (c - s)) % LANE, 2)
                acc = y if acc is None else jnp.where(slot == c, y, acc)
            out.append(jnp.concatenate([acc[g] for g in range(groups)], axis=-1))
    return out


def from_matrix(matrix, slot):
    count, rows, width = matrix.shape
    x = matrix.reshape(count // PER, PER, rows, width)
    out = []
    for g in range(width // LANE):
        part = lanes(x, g)
        for c in range(PER):
            acc = None
            for s in range(PER):
                y = part[:, s]
                if c != s:
                    y = pltpu.roll(y, (SLOT * (s - c)) % LANE, 2)
                acc = y if acc is None else jnp.where(slot == s, y, acc)
            out.append(acc)
    return out


def kernel(
    dims,
    mask, pair, cot, w_in, w_gate, w_out,
    update_out, grad_out,
    pad, proj, s1, r1, f1, s2, r2, bq, rb, bf, s3, r3, s4, r4, s5, r5, f5, s6, r6,
    gf, s7, r7, s8, r8, f8, s9, r9, su, ru, sg, rg,
    row_send, row_recv, col_send, col_recv, depth_send, depth_recv,
):
    n_d, n_r, n_c, i_block, k_block, ch, hid = dims
    i_q = i_block // n_d
    width = i_q * SLOT
    vl = width // LANE
    hr = hid // n_r
    me_d, me_r, me_c = lax.axis_index("depth"), lax.axis_index("row"), lax.axis_index("col")
    axes = {
        "row": (n_r, me_r, row_send, row_recv),
        "col": (n_c, me_c, col_send, col_recv),
        "depth": (n_d, me_d, depth_send, depth_recv),
    }

    barrier = pltpu.get_barrier_semaphore()
    for axis, (size, me, _, _) in axes.items():
        for o in range(1, size):
            pl.semaphore_signal(barrier, inc=1, device_id={axis: lax.rem(me + o, size)}, device_id_type=MESH)

    def copies(axis, phase, src_at, dst_at):
        size, me, send, recv = axes[axis]
        out = []
        for o in range(1, size):
            to = lax.rem(me + o, size)
            out.append((
                pltpu.make_async_remote_copy(
                    src_ref=src_at(to), dst_ref=dst_at(me), send_sem=send.at[phase, o], recv_sem=recv.at[phase, o],
                    device_id={axis: to}, device_id_type=MESH,
                ),
                pltpu.make_async_remote_copy(
                    src_ref=src_at(to), dst_ref=dst_at(lax.rem(me - o + size, size)), send_sem=send.at[phase, o],
                    recv_sem=recv.at[phase, o], device_id={axis: to}, device_id_type=MESH,
                ),
            ))
        return out

    started = []

    def start(axis, phase, src_at, dst_at):
        both = copies(axis, phase, src_at, dst_at)
        for go, _ in both:
            go.start()
        started.extend(both)
        return both

    def arrive(both):
        for _, come in both:
            come.wait_recv()

    slot = lax.broadcasted_iota(jnp.int32, (1, 1, LANE), 2) // SLOT

    def padded_t(ref):
        pad[:, :k_block, :] = ref[pl.ds(me_d * i_q, i_q)].astype(F32)
        pad[:, k_block:, :] = jnp.zeros((i_q, SLOT - k_block, ch), F32)
        return pad[...].reshape(width, ch).T

    x_hat, inv_std = norm_rows(padded_t(pair))
    normed = x_hat.astype(BF16)
    lane_id = lax.broadcasted_iota(jnp.int32, (1, width), 1)
    row_mask = jnp.zeros((1, width), F32)
    for i in range(i_q):
        here = mask[me_r * i_block + me_d * i_q + i].astype(F32)
        row_mask = jnp.where(lane_id // SLOT == i, here, row_mask)
    col_mask = jnp.zeros((1, width), F32)
    for t in range(k_block):
        here = mask[me_c * k_block + t].astype(F32)
        col_mask = jnp.where(lane_id % SLOT == t, here, col_mask)
    pair_mask = row_mask * col_mask
    w_in_t = w_in[...].astype(F32).T.astype(BF16)
    for block in range(2):
        both = dot(w_in_t[2 * block * hid : 2 * (block + 1) * hid], normed)
        sig, val = jax.nn.sigmoid(both[:hid]), both[hid:]
        proj[2 * block] = sig
        proj[2 * block + 1] = val
        s1[:, block * hr : (block + 1) * hr, :] = (pair_mask * sig * val).astype(BF16).reshape(n_r, hr, width)

    pl.semaphore_wait(barrier, (n_r - 1) + (n_c - 1) + (n_d - 1))
    move = start("row", 0, lambda t: s1.at[t], lambda t: r1.at[t])
    r1[me_r] = s1[me_r]
    cot_t = padded_t(cot)
    gate_val = jax.nn.sigmoid(dot(w_gate[...].astype(F32).T.astype(BF16), normed))
    w_out_t = w_out[...].astype(F32).T.astype(BF16)
    bf[...] = jnp.zeros_like(bf)
    arrive(move)

    x = r1[...].astype(F32)
    for v in range(vl):
        f1[v] = lanes(x, v).reshape(n_r * 2 * hr, LANE)
    for h in range(hr):
        for v in range(vl):
            a_rows = f1[v, pl.ds(h, n_r, stride=2 * hr), :]
            b_rows = f1[v, pl.ds(hr + h, n_r, stride=2 * hr), :]
            s2[h, :, v * LANE : (v + 1) * LANE] = jnp.concatenate([a_rows, b_rows], axis=0).astype(BF16)
    move = start("col", 0, lambda t: s2.at[t], lambda t: r2.at[t])
    r2[me_c] = s2[me_c]
    arrive(move)

    x = r2[...].astype(F32)
    ab = to_matrix([lanes(x, v) for v in range(vl)], slot)
    bq[...] = jnp.concatenate([m[n_r:] for m in ab], axis=0).astype(BF16)
    move = start("depth", 0, lambda t: bq, lambda t: rb.at[t])
    rb[me_d] = bq[...]
    a_mat = jnp.concatenate([m[:n_r] for m in ab], axis=0).astype(BF16)
    arrive(move)

    per_row = i_block // k_block
    groups = n_c * SLOT // LANE

    def strided(d, i):
        at = d * i_q + i
        return pl.ds(SLOT * (at // k_block) + at % k_block, n_r, stride=SLOT * per_row)

    for d in range(n_d):
        x = rb[d].astype(F32)
        for i in range(i_q):
            for g in range(groups):
                bf[g, strided(d, i), :] = lanes(x[i * n_r : (i + 1) * n_r], g)
    b_mat = jnp.concatenate([bf[g].astype(BF16) for g in range(groups)], axis=-1)
    tri = lax.dot_general(a_mat, b_mat, (((1,), (1,)), ((), ())), preferred_element_type=F32)

    for c, x in enumerate(from_matrix(tri.reshape(i_q, n_r, n_c * SLOT), slot)):
        s3[c] = x.reshape(vl * n_r, LANE)
    size3 = vl * n_r

    def part3(ref):
        return lambda t: ref.at[pl.ds(pl.multiple_of(t * size3, size3), size3)]

    move = start("col", 1, lambda t: s3.at[t], part3(r3))
    r3[pl.ds(pl.multiple_of(me_c * size3, size3), size3), :] = s3[me_c]
    arrive(move)
    for r in range(n_r):
        for v in range(vl):
            s4[r, :, v * LANE : (v + 1) * LANE] = r3[pl.ds(v * n_r + r, n_c, stride=size3), :].astype(BF16)
    move = start("row", 1, lambda t: s4.at[t], lambda t: r4.at[t])
    r4[me_r] = s4[me_r]
    arrive(move)

    y_hat, tri_std = norm_rows(r4[...].astype(F32).reshape(hid, width))
    out_proj = dot(w_out_t, y_hat.astype(BF16))
    d_o = (cot_t * gate_val).astype(BF16)
    d_y = dot(w_out[...], d_o)
    tri_grad = norm_back(y_hat, tri_std, d_y)
    s5[...] = tri_grad.astype(BF16).reshape(n_r, hr, width)
    move = start("row", 2, lambda t: s5.at[t], lambda t: r5.at[t])
    r5[me_r] = s5[me_r]

    def natural(x):
        return x.T.reshape(i_q, SLOT, ch)[:, :k_block, :].reshape(i_q * k_block, ch).astype(BF16)

    su[...] = natural(gate_val * out_proj)
    update_move = start("depth", 1, lambda t: su, lambda t: ru.at[t])
    ru[me_d] = su[...]
    d_gate_pre = (cot_t * out_proj * gate_val * (1.0 - gate_val)).astype(BF16)
    d_gate = dot(w_gate[...], d_gate_pre)
    arrive(move)

    x = r5[...].astype(F32)
    for v in range(vl):
        f5[v] = lanes(x, v).reshape(n_r * hr, LANE)
    for h in range(hr):
        for v in range(vl):
            s6[h, v * n_r : (v + 1) * n_r, :] = f5[v, pl.ds(h, n_r, stride=hr), :]
    move = start("col", 2, lambda t: s6.at[t], lambda t: r6.at[t])
    r6[me_c] = s6[me_c]
    arrive(move)
    tg = jnp.concatenate(to_matrix([r6[:, v * n_r : (v + 1) * n_r, :] for v in range(vl)], slot), axis=0)
    tg_t = tg.T.astype(BF16)
    part_b = dot(tg_t, a_mat)
    for g in range(groups):
        gf[g] = lanes(part_b, g)
    for d in range(n_d):
        s7[d] = jnp.concatenate(
            [
                jnp.concatenate([gf[g, strided(d, i), :] for g in range(groups)], axis=-1)
                for i in range(i_q)
            ],
            axis=0,
        ).astype(BF16)
    move = start("depth", 2, lambda t: s7.at[t], lambda t: r7.at[t])
    r7[me_d] = s7[me_d]
    grad_a = dot(tg.astype(BF16), b_mat)
    arrive(move)
    grad_b = r7[0].astype(F32)
    for d in range(1, n_d):
        grad_b = grad_b + r7[d].astype(F32)

    both = jnp.concatenate(
        [grad_a.reshape(i_q, n_r, n_c * SLOT), grad_b.reshape(i_q, n_r, n_c * SLOT)], axis=1
    )
    for c, x in enumerate(from_matrix(both, slot)):
        for v in range(vl):
            s8[c, :, v * LANE : (v + 1) * LANE] = x[v].astype(BF16)
    move = start("col", 3, lambda t: s8.at[t], lambda t: r8.at[t])
    r8[me_c] = s8[me_c]
    arrive(move)
    x = r8[...].astype(F32)
    for v in range(vl):
        f8[v] = lanes(x, v).reshape(n_c * 2 * n_r, LANE)
    for r in range(n_r):
        for v in range(vl):
            for block in range(2):
                s9[r, block * hr : (block + 1) * hr, v * LANE : (v + 1) * LANE] = f8[
                    v, pl.ds(block * n_r + r, n_c, stride=2 * n_r), :
                ].astype(BF16)
    move = start("row", 3, lambda t: s9.at[t], lambda t: r9.at[t])
    r9[me_r] = s9[me_r]
    arrive(move)

    d_normed = d_gate
    for block in range(2):
        grad = r9[:, block * hr : (block + 1) * hr, :].astype(F32).reshape(hid, width) * pair_mask
        sig, val = proj[2 * block], proj[2 * block + 1]
        d_pre = (grad * val * sig * (1.0 - sig)).astype(BF16)
        d_val = (grad * sig).astype(BF16)
        d_normed = d_normed + dot(w_in[:, 2 * block * hid : (2 * block + 1) * hid], d_pre)
        d_normed = d_normed + dot(w_in[:, (2 * block + 1) * hid : (2 * block + 2) * hid], d_val)
    sg[...] = natural(norm_back(x_hat, inv_std, d_normed))
    move = start("depth", 3, lambda t: sg, lambda t: rg.at[t])
    rg[me_d] = sg[...]
    arrive(update_move)
    for d in range(n_d):
        update_out[d * i_q : (d + 1) * i_q] = ru[d].astype(F32).reshape(i_q, k_block, ch).astype(BF16)
    arrive(move)
    for d in range(n_d):
        grad_out[d * i_q : (d + 1) * i_q] = rg[d].astype(F32).reshape(i_q, k_block, ch).astype(BF16)
    for go, _ in started:
        go.wait_send()


def shards(sizes, pair, cotangent, w_in, w_gate, w_out, residue_mask):
    n_d, n_r, n_c = sizes
    i_block, k_block, ch = pair.shape
    hid = w_out.shape[0]
    i_q = i_block // n_d
    width = i_q * SLOT
    vl = width // LANE
    hr = hid // n_r
    groups = n_c * SLOT // LANE
    rows_q = i_q * n_r
    full = n_c * SLOT
    vm = pltpu.VMEM
    scratch = [
        vm((i_q, SLOT, ch), F32),
        vm((4, hid, width), F32),
        vm((n_r, 2 * hr, width), BF16),
        vm((n_r, 2 * hr, width), BF16),
        vm((vl, n_r * 2 * hr, LANE), F32),
        vm((n_c, 2 * n_r, width), BF16),
        vm((n_c, 2 * n_r, width), BF16),
        vm((rows_q, full), BF16),
        vm((n_d, rows_q, full), BF16),
        vm((groups, full, LANE), F32),
        vm((n_c, vl * n_r, LANE), F32),
        vm((n_c * vl * n_r, LANE), F32),
        vm((n_r, hr, width), BF16),
        vm((n_r, hr, width), BF16),
        vm((n_r, hr, width), BF16),
        vm((n_r, hr, width), BF16),
        vm((vl, n_r * hr, LANE), F32),
        vm((n_c, vl * n_r, LANE), F32),
        vm((n_c, vl * n_r, LANE), F32),
        vm((groups, full, LANE), F32),
        vm((n_d, rows_q, full), BF16),
        vm((n_d, rows_q, full), BF16),
        vm((n_c, 2 * n_r, width), BF16),
        vm((n_c, 2 * n_r, width), BF16),
        vm((vl, n_c * 2 * n_r, LANE), F32),
        vm((n_r, 2 * hr, width), BF16),
        vm((n_r, 2 * hr, width), BF16),
        vm((i_q * k_block, ch), BF16),
        vm((n_d, i_q * k_block, ch), BF16),
        vm((i_q * k_block, ch), BF16),
        vm((n_d, i_q * k_block, ch), BF16),
    ]
    for size in (n_r, n_c, n_d):
        scratch += [pltpu.SemaphoreType.DMA((4, size))] * 2
    whole = pl.BlockSpec(memory_space=pltpu.VMEM)
    return pl.pallas_call(
        functools.partial(kernel, (n_d, n_r, n_c, i_block, k_block, ch, hid)),
        out_shape=(jax.ShapeDtypeStruct(pair.shape, BF16),) * 2,
        in_specs=[pl.BlockSpec(memory_space=pltpu.SMEM)] + [whole] * 5,
        out_specs=(whole, whole),
        scratch_shapes=scratch,
        compiler_params=pltpu.CompilerParams(
            collective_id=0, has_side_effects=True, vmem_limit_bytes=40 * 1024 * 1024
        ),
    )(residue_mask, pair, cotangent, w_in, w_gate, w_out)


def solution(mesh):
    in_specs = (P("row", "col", None), P("row", "col", None), P(), P(), P(), P())
    out_specs = (P("row", "col", None), P("row", "col", None))
    sizes = (mesh.shape["depth"], mesh.shape["row"], mesh.shape["col"])
    return jax.shard_map(
        functools.partial(shards, sizes), mesh=mesh, in_specs=in_specs, out_specs=out_specs, check_vma=False
    )
```

```python
import functools

import jax
import jax.numpy as jnp
from jax import lax
from jax.experimental import pallas as pl
from jax.experimental.pallas import tpu as pltpu
from jax.sharding import PartitionSpec as P

MESH = pl.DeviceIdType.MESH
F32 = jnp.float32
BF16 = jnp.bfloat16
SLOT = 32
LANE = 128
PER = LANE // SLOT


def dot(left, right):
    return jnp.dot(left, right, preferred_element_type=F32)


def norm_rows(values):
    average = jnp.mean(values, axis=0, keepdims=True)
    centered = values - average
    variance = jnp.mean(centered * centered, axis=0, keepdims=True)
    inv_std = lax.rsqrt(variance + 1e-05)
    return (centered * inv_std, inv_std)


def norm_back(x_hat, inv_std, upstream):
    first = jnp.mean(upstream, axis=0, keepdims=True)
    second = jnp.mean(upstream * x_hat, axis=0, keepdims=True)
    return inv_std * (upstream - first - x_hat * second)


def lanes(x, v):
    return x[..., v * LANE : (v + 1) * LANE]


def to_matrix(tiles, slot):
    out = []
    for x in tiles:
        groups, rows = x.shape[0] // PER, x.shape[1]
        x = x.reshape(groups, PER, rows, LANE)
        for s in range(PER):
            acc = None
            for c in range(PER):
                y = x[:, c]
                if c != s:
                    y = pltpu.roll(y, (SLOT * (c - s)) % LANE, 2)
                acc = y if acc is None else jnp.where(slot == c, y, acc)
            out.append(jnp.concatenate([acc[g] for g in range(groups)], axis=-1))
    return out


def from_matrix(matrix, slot):
    count, rows, width = matrix.shape
    x = matrix.reshape(count // PER, PER, rows, width)
    out = []
    for g in range(width // LANE):
        part = lanes(x, g)
        for c in range(PER):
            acc = None
            for s in range(PER):
                y = part[:, s]
                if c != s:
                    y = pltpu.roll(y, (SLOT * (s - c)) % LANE, 2)
                acc = y if acc is None else jnp.where(slot == s, y, acc)
            out.append(acc)
    return out


def kernel(
    dims,
    mask_hbm, pair_hbm, cot_hbm, w_in_hbm, w_gate_hbm, w_out_hbm,
    update_out, grad_out,
    mask, pair, cot, w_in, w_gate, w_out, in_sem,
    pad, proj, s1, r1, f1, s2, r2, bn, s3, r3, s4, r4, s5, r5, f5, s6, r6, tgf,
    gf, s8, r8, f8, s9, r9, su, ru, sg, rg,
    z_send, z_recv, col_send, col_recv, depth_send, depth_recv,
):
    n_d, n_r, n_c, n_x, i_block, k_block, ch, hid = dims
    n_zh, n_dd, n_y = n_r // 2, n_d // 2, n_c // n_x
    n_z = n_zh * n_d
    hz = hid // n_z
    i_q = i_block // n_d
    width = i_q * SLOT
    vl = width // LANE
    half = 2 * n_zh
    full = n_c * SLOT
    groups = full // LANE
    me_d, me_r, me_c = lax.axis_index("depth"), lax.axis_index("row"), lax.axis_index("col")
    me_zh, me_core = me_r // 2, me_r % 2

    def z_slot(zh, d):
        return (d % n_dd) * half + (d // n_dd) * n_zh + zh

    def c_slot(c):
        return ((c // 2) % 2) * half + (c % 2) * n_zh + c // 4

    me_s, me_p = z_slot(me_zh, me_d), c_slot(me_c)
    me_dd = me_p % 2

    def z_peer(o):
        z = lax.rem(me_zh * n_d + me_d + o + n_z, n_z)
        zh, d = z // n_d, z % n_d
        return {"row": zh * 2 + me_core, "depth": d}, z_slot(zh, d)

    def c_peer(core, ox, oy):
        x = lax.rem(me_c // n_y + ox + n_x, n_x)
        y = lax.rem(me_c % n_y + oy + n_y, n_y)
        c = x * n_y + y
        return {"row": me_zh * 2 + core, "col": c}, c_slot(c)

    def d_peer(o):
        d = lax.rem(me_d + o + n_d, n_d)
        return {"depth": d}, d

    z_offsets = sorted(range(1, n_z), key=lambda o: -min(o, n_z - o))
    c_offsets = sorted(
        [(x, y) for x in range(n_x) for y in range(n_y)],
        key=lambda o: -(min(o[0], n_x - o[0]) + min(o[1], n_y - o[1])),
    )
    d_offsets = list(range(1, n_d))

    z_list = [z_peer(o) + (z_peer(-o)[1], k) for k, o in enumerate(z_offsets)]
    d_list = [d_peer(o) + (d_peer(-o)[1], k) for k, o in enumerate(d_offsets)]
    c_same, c_other = [], []
    for k, (ox, oy) in enumerate(c_offsets):
        if (ox, oy) != (0, 0):
            c_same.append(c_peer(me_core, ox, oy) + (c_peer(me_core, -ox, -oy)[1], k))
        c_other.append(c_peer(1 - me_core, ox, oy) + (c_peer(me_core, -ox, -oy)[1], n_c + k))

    barrier = pltpu.get_barrier_semaphore()
    peers = z_list + c_same + c_other
    for to, _, _, _ in peers:
        pl.semaphore_signal(barrier, inc=1, device_id=to, device_id_type=MESH)

    own_rows = pl.ds(me_d * i_q, i_q)
    fetch = [
        pltpu.make_async_copy(a, b, in_sem.at[k])
        for k, (a, b) in enumerate([
            (pair_hbm.at[own_rows], pair), (w_in_hbm, w_in), (mask_hbm, mask),
            (cot_hbm.at[own_rows], cot), (w_gate_hbm, w_gate), (w_out_hbm, w_out),
        ])
    ]
    for f in fetch:
        f.start()

    started = []

    def start(peer_list, send, recv, src_at, dst_mine, dst_from):
        both = []
        for to, slot_to, slot_from, k in peer_list:
            go = pltpu.make_async_remote_copy(
                src_ref=src_at(slot_to), dst_ref=dst_mine, send_sem=send.at[k], recv_sem=recv.at[k],
                device_id=to, device_id_type=MESH,
            )
            come = pltpu.make_async_remote_copy(
                src_ref=src_at(slot_to), dst_ref=dst_from(slot_from), send_sem=send.at[k], recv_sem=recv.at[k],
                device_id=to, device_id_type=MESH,
            )
            go.start()
            both.append((go, come))
        started.extend(both)
        return both

    def arrive(both):
        for _, come in both:
            come.wait_recv()

    def start_z(phase, s, r):
        both = start(z_list, z_send.at[phase], z_recv.at[phase], lambda t: s.at[t], r.at[me_s], lambda t: r.at[t])
        r[me_s] = s[me_s]
        return both

    def start_c(phase, s, r):
        both = start(c_same, col_send.at[phase], col_recv.at[phase], lambda t: s.at[t], r.at[me_p], lambda t: r.at[t])
        r[me_p] = s[me_p]
        return both

    def start_cc(phase, s, r):
        sems = (col_send.at[phase], col_recv.at[phase])
        both = start(c_same, *sems, lambda t: s.at[t], r.at[me_core, me_p], lambda t: r.at[me_core, t])
        both += start(c_other, *sems, lambda t: s.at[t], r.at[me_core, me_p], lambda t: r.at[1 - me_core, t])
        r[me_core, me_p] = s[me_p]
        return both

    def start_d(phase, s, r):
        both = start(d_list, depth_send.at[phase], depth_recv.at[phase], lambda t: s, r.at[me_d], lambda t: r.at[t])
        r[me_d] = s[...]
        return both

    slot = lax.broadcasted_iota(jnp.int32, (1, 1, LANE), 2) // SLOT

    def padded_t(ref):
        pad[:, :k_block, :] = ref[...].astype(F32)
        pad[:, k_block:, :] = jnp.zeros((i_q, SLOT - k_block, ch), F32)
        return pad[...].reshape(width, ch).T

    def pack(x):
        parts = [lanes(x, v).reshape(n_z, hz, LANE) for v in range(vl)]
        short = s5.shape[1] - vl * hz
        if short:
            parts.append(jnp.zeros((n_z, short, LANE), F32))
        return jnp.concatenate(parts, axis=1).astype(BF16)

    fetch[0].wait()
    x_hat, inv_std = norm_rows(padded_t(pair))
    normed = x_hat.astype(BF16)
    fetch[1].wait()
    w_in_t = w_in[...].astype(F32).T.astype(BF16)
    fetch[2].wait()
    lane_id = lax.broadcasted_iota(jnp.int32, (1, width), 1)
    row_mask = jnp.zeros((1, width), F32)
    for i in range(i_q):
        here = mask[me_r * i_block + me_d * i_q + i].astype(F32)
        row_mask = jnp.where(lane_id // SLOT == i, here, row_mask)
    col_mask = jnp.zeros((1, width), F32)
    for t in range(k_block):
        here = mask[me_c * k_block + t].astype(F32)
        col_mask = jnp.where(lane_id % SLOT == t, here, col_mask)
    pair_mask = row_mask * col_mask
    parts = []
    for block in range(2):
        both = dot(w_in_t[2 * block * hid : 2 * (block + 1) * hid], normed)
        sig, val = jax.nn.sigmoid(both[:hid]), both[hid:]
        proj[2 * block] = sig
        proj[2 * block + 1] = val
        parts.append((pair_mask * sig * val).reshape(n_z, hz, width))
    s1[...] = jnp.concatenate(parts, axis=1).astype(BF16)

    pl.semaphore_wait(barrier, len(peers))
    move = start_z(0, s1, r1)
    for f in fetch[3:]:
        f.wait()
    cot_t = padded_t(cot)
    gate_val = jax.nn.sigmoid(dot(w_gate[...].astype(F32).T.astype(BF16), normed))
    w_out_t = w_out[...].astype(F32).T.astype(BF16)
    arrive(move)

    x = r1[...].astype(F32)
    for v in range(vl):
        f1[v] = lanes(x, v).reshape(n_z * 2 * hz, LANE)
    for h in range(hz):
        for v in range(vl):
            a0, b0, a1, b1 = (
                f1[v, pl.ds(dd * half * 2 * hz + block * hz + h, half, stride=2 * hz), :]
                for dd in range(2) for block in range(2)
            )
            at = slice(v * LANE, (v + 1) * LANE)
            s2[2 * h, :, at] = jnp.concatenate([a0, a1, b0, b1], axis=0).astype(BF16)
            s2[2 * h + 1, :, at] = jnp.concatenate([a1, a0, b0, b1], axis=0).astype(BF16)
    move = start_cc(0, s2, r2)
    arrive(move)

    for core in range(2):
        x = r2[core, :, 2 * half :, :].astype(F32)
        for i, m in enumerate(to_matrix([lanes(x, v) for v in range(vl)], slot)):
            for dd in range(n_dd):
                at = ((core * n_dd + dd) * i_q + i) * half
                for g in range(groups):
                    bn[g, at : at + half, :] = lanes(m[dd * half : (dd + 1) * half], g)
    rows = []
    for core in range(2):
        for q in range(half):
            rows.append(jnp.concatenate(
                [bn[g, pl.ds(core * k_block * half + q, k_block, stride=half), :] for g in range(groups)], axis=-1
            ))
            rows.append(jnp.zeros((SLOT - k_block, full), F32))
    b_mat = jnp.concatenate(rows, axis=0).astype(BF16)
    x = r2[me_core, :, :half, :].astype(F32)
    a_own = jnp.concatenate(to_matrix([lanes(x, v) for v in range(vl)], slot), axis=0).astype(BF16)
    tri = lax.dot_general(a_own, b_mat, (((1,), (1,)), ((), ())), preferred_element_type=F32)
    for c, x in enumerate(from_matrix(tri.reshape(i_q, half, full), slot)):
        s3[c] = x.reshape(vl * half, LANE)
    size3 = vl * half

    def rows3(t):
        return pl.ds(pl.multiple_of(t * size3, size3), size3)

    move = start(
        c_same, col_send.at[1], col_recv.at[1], lambda t: s3.at[t], r3.at[rows3(me_p)], lambda t: r3.at[rows3(t)]
    )
    r3[rows3(me_p), :] = s3[me_p]

    rows = []
    for core in range(2):
        x = r2[core, :, : 2 * half, :].astype(F32)
        rows += to_matrix([lanes(x, v) for v in range(vl)], slot)
    a_mat = jnp.concatenate(rows, axis=0).astype(BF16)
    arrive(move)

    for dd in range(n_dd):
        for q in range(half):
            parts = [r3[pl.ds(dd * size3 + v * half + q, hz, stride=2 * size3), :] for v in range(vl)]
            short = s4.shape[1] - vl * hz
            if short:
                parts.append(jnp.zeros((short, LANE), F32))
            s4[dd * half + q] = jnp.concatenate(parts, axis=0).astype(BF16)
    move = start_z(1, s4, r4)
    arrive(move)

    x = r4[...].astype(F32)
    tri_t = jnp.concatenate([x[:, v * hz : (v + 1) * hz, :].reshape(hid, LANE) for v in range(vl)], axis=-1)
    y_hat, tri_std = norm_rows(tri_t)
    out_proj = dot(w_out_t, y_hat.astype(BF16))
    d_o = (cot_t * gate_val).astype(BF16)
    d_y = dot(w_out[...], d_o)
    s5[...] = pack(norm_back(y_hat, tri_std, d_y))
    move = start_z(2, s5, r5)

    def natural(x):
        return x.T.reshape(i_q, SLOT, ch)[:, :k_block, :].reshape(i_q * k_block, ch).astype(BF16)

    su[...] = natural(gate_val * out_proj)
    update_move = start_d(0, su, ru)
    d_gate_pre = (cot_t * out_proj * gate_val * (1.0 - gate_val)).astype(BF16)
    d_gate = dot(w_gate[...], d_gate_pre)
    arrive(move)

    pitch = s5.shape[1]
    f5[...] = r5[...].astype(F32).reshape(n_z * pitch, LANE)
    for h in range(hz):
        for v in range(vl):
            t0, t1 = (f5[pl.ds(dd * half * pitch + v * hz + h, half, stride=pitch), :] for dd in range(2))
            at = slice(v * LANE, (v + 1) * LANE)
            s6[2 * h, :, at] = jnp.concatenate([t0, t1], axis=0).astype(BF16)
            s6[2 * h + 1, :, at] = jnp.concatenate([t1, t0], axis=0).astype(BF16)
    move = start_cc(2, s6, r6)
    arrive(move)
    for core in range(2):
        x = r6[core].astype(F32)
        for i, m in enumerate(to_matrix([lanes(x, v) for v in range(vl)], slot)):
            tgf[core, i] = m
    tg_own = tgf[me_core, :, :half, :].reshape(i_q * half, full).astype(BF16)
    mine = pl.ds(pl.multiple_of(me_core * (full // 2), full // 2), full // 2)
    tg_t = tgf[:, :, :, mine].reshape(2 * i_q * 2 * half, full // 2).T.astype(BF16)
    part_b = dot(tg_t, a_mat)
    for g in range(groups):
        gf[g] = lanes(part_b, g)
    grad_a = dot(tg_own, b_mat).reshape(i_q, half, full)
    rows = []
    for i in range(i_q):
        rows.append(grad_a[i])
        rows.append(jnp.concatenate(
            [gf[g, pl.ds(me_dd * i_q + i, half, stride=SLOT), :] for g in range(groups)], axis=-1
        ))
    both = jnp.concatenate(rows, axis=0).reshape(i_q, 2 * half, full)
    for c, x in enumerate(from_matrix(both, slot)):
        for v in range(vl):
            s8[c, :, v * LANE : (v + 1) * LANE] = x[v].astype(BF16)
    move = start_c(3, s8, r8)
    arrive(move)
    x = r8[...].astype(F32)
    for v in range(vl):
        f8[v] = lanes(x, v).reshape(n_c * 2 * half, LANE)
    for dd in range(n_dd):
        for q in range(half):
            for v in range(vl):
                s9[dd * half + q, :, v * LANE : (v + 1) * LANE] = jnp.concatenate(
                    [
                        f8[v, pl.ds((dd * 2 + block) * half + q, hz, stride=4 * half), :]
                        for block in range(2)
                    ],
                    axis=0,
                ).astype(BF16)
    move = start_z(3, s9, r9)
    arrive(move)

    d_normed = d_gate
    x = r9[...].astype(F32)
    for block in range(2):
        grad = x[:, block * hz : (block + 1) * hz, :].reshape(hid, width) * pair_mask
        sig, val = proj[2 * block], proj[2 * block + 1]
        d_pre = (grad * val * sig * (1.0 - sig)).astype(BF16)
        d_val = (grad * sig).astype(BF16)
        d_normed = d_normed + dot(w_in[:, 2 * block * hid : (2 * block + 1) * hid], d_pre)
        d_normed = d_normed + dot(w_in[:, (2 * block + 1) * hid : (2 * block + 2) * hid], d_val)
    sg[...] = natural(norm_back(x_hat, inv_std, d_normed))
    move = start_d(1, sg, rg)
    arrive(update_move)
    for d in range(n_d):
        update_out[d * i_q : (d + 1) * i_q] = ru[d].astype(F32).reshape(i_q, k_block, ch).astype(BF16)
    arrive(move)
    for d in range(n_d):
        grad_out[d * i_q : (d + 1) * i_q] = rg[d].astype(F32).reshape(i_q, k_block, ch).astype(BF16)
    for go, _ in started:
        go.wait_send()


def shards(sizes, pair, cotangent, w_in, w_gate, w_out, residue_mask):
    n_d, n_r, n_c = sizes
    n_x = 4 if n_c == 16 else 2
    i_block, k_block, ch = pair.shape
    hid = w_out.shape[0]
    i_q = i_block // n_d
    width = i_q * SLOT
    vl = width // LANE
    n_z = (n_r // 2) * n_d
    half = n_r
    hz = hid // n_z
    full = n_c * SLOT
    groups = max(full // LANE, 1)
    pitch = -(-vl * hz // 16) * 16
    vm = pltpu.VMEM
    scratch = [
        pltpu.SMEM(residue_mask.shape, jnp.int32),
        vm((i_q, k_block, ch), BF16),
        vm((i_q, k_block, ch), BF16),
        vm(w_in.shape, BF16),
        vm(w_gate.shape, BF16),
        vm(w_out.shape, BF16),
        pltpu.SemaphoreType.DMA((6,)),
        vm((i_q, SLOT, ch), F32),
        vm((4, hid, width), F32),
        vm((n_z, 2 * hz, width), BF16),
        vm((n_z, 2 * hz, width), BF16),
        vm((vl, n_z * 2 * hz, LANE), F32),
        vm((n_c, 4 * half, width), BF16),
        vm((2, n_c, 4 * half, width), BF16),
        vm((groups, 2 * k_block * half, LANE), F32),
        vm((n_c, vl * half, LANE), F32),
        vm((n_c * vl * half, LANE), F32),
        vm((n_z, pitch, LANE), BF16),
        vm((n_z, pitch, LANE), BF16),
        vm((n_z, pitch, LANE), BF16),
        vm((n_z, pitch, LANE), BF16),
        vm((n_z * pitch, LANE), F32),
        vm((n_c, 2 * half, width), BF16),
        vm((2, n_c, 2 * half, width), BF16),
        vm((2, i_q, 2 * half, full), F32),
        vm((groups, full // 2, LANE), F32),
        vm((n_c, 2 * half, width), BF16),
        vm((n_c, 2 * half, width), BF16),
        vm((vl, n_c * 2 * half, LANE), F32),
        vm((n_z, 2 * hz, width), BF16),
        vm((n_z, 2 * hz, width), BF16),
        vm((i_q * k_block, ch), BF16),
        vm((n_d, i_q * k_block, ch), BF16),
        vm((i_q * k_block, ch), BF16),
        vm((n_d, i_q * k_block, ch), BF16),
    ]
    for phases, size in ((4, n_z), (4, 2 * n_c), (2, n_d)):
        scratch += [pltpu.SemaphoreType.DMA((phases, size))] * 2
    whole = pl.BlockSpec(memory_space=pltpu.VMEM)
    return pl.pallas_call(
        functools.partial(kernel, (n_d, n_r, n_c, n_x, i_block, k_block, ch, hid)),
        out_shape=(jax.ShapeDtypeStruct(pair.shape, BF16),) * 2,
        in_specs=[pl.BlockSpec(memory_space=pl.ANY)] * 6,
        out_specs=(whole, whole),
        scratch_shapes=scratch,
        compiler_params=pltpu.CompilerParams(
            collective_id=0, has_side_effects=True, vmem_limit_bytes=60 * 1024 * 1024
        ),
    )(residue_mask, pair, cotangent, w_in, w_gate, w_out)


def solution(mesh):
    in_specs = (P("row", "col", None), P("row", "col", None), P(), P(), P(), P())
    out_specs = (P("row", "col", None), P("row", "col", None))
    sizes = (mesh.shape["depth"], mesh.shape["row"], mesh.shape["col"])
    return jax.shard_map(
        functools.partial(shards, sizes), mesh=mesh, in_specs=in_specs, out_specs=out_specs, check_vma=False
    )
```

```python
import functools

import jax
import jax.numpy as jnp
from jax import lax
from jax.experimental import pallas as pl
from jax.experimental.pallas import tpu as pltpu
from jax.sharding import PartitionSpec as P

MESH = pl.DeviceIdType.MESH
F32 = jnp.float32
BF16 = jnp.bfloat16
SLOT = 32
LANE = 128
PER = LANE // SLOT


def dot(left, right):
    return jnp.dot(left, right, preferred_element_type=F32)


def norm_rows(values):
    average = jnp.mean(values, axis=0, keepdims=True)
    centered = values - average
    variance = jnp.mean(centered * centered, axis=0, keepdims=True)
    inv_std = lax.rsqrt(variance + 1e-05)
    return (centered * inv_std, inv_std)


def norm_back(x_hat, inv_std, upstream):
    first = jnp.mean(upstream, axis=0, keepdims=True)
    second = jnp.mean(upstream * x_hat, axis=0, keepdims=True)
    return inv_std * (upstream - first - x_hat * second)


def lanes(x, v):
    return x[..., v * LANE : (v + 1) * LANE]


def to_matrix(tiles, slot):
    out = []
    for x in tiles:
        groups, rows = x.shape[0] // PER, x.shape[1]
        x = x.reshape(groups, PER, rows, LANE)
        for s in range(PER):
            acc = None
            for c in range(PER):
                y = x[:, c]
                if c != s:
                    y = pltpu.roll(y, (SLOT * (c - s)) % LANE, 2)
                acc = y if acc is None else jnp.where(slot == c, y, acc)
            out.append(jnp.concatenate([acc[g] for g in range(groups)], axis=-1))
    return out


def from_matrix(matrix, slot):
    count, rows, width = matrix.shape
    x = matrix.reshape(count // PER, PER, rows, width)
    out = []
    for g in range(width // LANE):
        part = lanes(x, g)
        for c in range(PER):
            acc = None
            for s in range(PER):
                y = part[:, s]
                if c != s:
                    y = pltpu.roll(y, (SLOT * (s - c)) % LANE, 2)
                acc = y if acc is None else jnp.where(slot == s, y, acc)
            out.append(acc)
    return out


def kernel(
    dims,
    mask_hbm, pair_hbm, cot_hbm, w_in_hbm, w_gate_hbm, w_out_hbm,
    update_out, grad_out,
    mask, pair, cot, w_in, w_gate, w_out, in_sem,
    pad, proj, s1, r1, f1, s2a, s2b, r2a, r2b, bn, s3, r3, s4, r4, s5, r5, f5, s6, r6, tgf,
    gf, s8, r8, f8, s9, r9, su, ru, sg, rg,
    z_send, z_recv, col_send, col_recv, depth_send, depth_recv, twin_send, twin_recv,
):
    n_d, n_r, n_c, n_x, i_block, k_block, ch, hid = dims
    n_zh, n_dd, n_y = n_r // 2, n_d // 2, n_c // n_x
    n_z = n_zh * n_d
    hz = hid // n_z
    i_q = i_block // n_d
    width = i_q * SLOT
    vl = width // LANE
    half = 2 * n_zh
    full = n_c * SLOT
    groups = full // LANE
    me_d, me_r, me_c = lax.axis_index("depth"), lax.axis_index("row"), lax.axis_index("col")
    me_zh, me_core = me_r // 2, me_r % 2

    def z_slot(zh, d):
        return (d % n_dd) * half + (d // n_dd) * n_zh + zh

    def c_slot(c):
        return ((c // 2) % 2) * half + (c % 2) * n_zh + c // 4

    me_s, me_p = z_slot(me_zh, me_d), c_slot(me_c)
    me_dd = me_p % 2

    def z_peer(o):
        z = lax.rem(me_zh * n_d + me_d + o + n_z, n_z)
        zh, d = z // n_d, z % n_d
        return {"row": zh * 2 + me_core, "depth": d}, z_slot(zh, d)

    def c_peer(ox, oy):
        x = lax.rem(me_c // n_y + ox + n_x, n_x)
        y = lax.rem(me_c % n_y + oy + n_y, n_y)
        c = x * n_y + y
        return {"col": c}, c_slot(c)

    def d_peer(o):
        d = lax.rem(me_d + o + n_d, n_d)
        return {"depth": d}, d

    z_offsets = sorted(range(1, n_z), key=lambda o: -min(o, n_z - o))
    c_offsets = sorted(
        [(x, y) for x in range(n_x) for y in range(n_y)],
        key=lambda o: -(min(o[0], n_x - o[0]) + min(o[1], n_y - o[1])),
    )
    d_offsets = list(range(1, n_d))

    z_list = [z_peer(o) + (z_peer(-o)[1], k) for k, o in enumerate(z_offsets)]
    d_list = [d_peer(o) + (d_peer(-o)[1], k) for k, o in enumerate(d_offsets)]
    c_list = [
        c_peer(ox, oy) + (c_peer(-ox, -oy)[1], k) for k, (ox, oy) in enumerate(c_offsets) if (ox, oy) != (0, 0)
    ]
    twin = {"row": me_zh * 2 + 1 - me_core}

    barrier = pltpu.get_barrier_semaphore()
    peers = [to for to, _, _, _ in z_list + c_list] + [twin]
    for to in peers:
        pl.semaphore_signal(barrier, inc=1, device_id=to, device_id_type=MESH)

    own_rows = pl.ds(me_d * i_q, i_q)
    fetch = [
        pltpu.make_async_copy(a, b, in_sem.at[k])
        for k, (a, b) in enumerate([
            (pair_hbm.at[own_rows], pair), (w_in_hbm, w_in), (mask_hbm, mask),
            (cot_hbm.at[own_rows], cot), (w_gate_hbm, w_gate), (w_out_hbm, w_out),
        ])
    ]
    for f in fetch:
        f.start()

    started = []

    def start(peer_list, send, recv, src_at, dst_mine, dst_from):
        both = []
        for to, slot_to, slot_from, k in peer_list:
            go = pltpu.make_async_remote_copy(
                src_ref=src_at(slot_to), dst_ref=dst_mine, send_sem=send.at[k], recv_sem=recv.at[k],
                device_id=to, device_id_type=MESH,
            )
            come = pltpu.make_async_remote_copy(
                src_ref=src_at(slot_to), dst_ref=dst_from(slot_from), send_sem=send.at[k], recv_sem=recv.at[k],
                device_id=to, device_id_type=MESH,
            )
            go.start()
            both.append((go, come))
        started.extend(both)
        return both

    def arrive(both):
        for _, come in both:
            come.wait_recv()

    def start_z(phase, s, r):
        both = start(z_list, z_send.at[phase], z_recv.at[phase], lambda t: s.at[t], r.at[me_s], lambda t: r.at[t])
        r[me_s] = s[me_s]
        return both

    def start_c(phase, src_at, dst_at, own):
        both = start(c_list, col_send.at[phase], col_recv.at[phase], src_at, dst_at(me_p), dst_at)
        own()
        return both

    def pass_on(number, k, ref_at):
        sems = {"send_sem": twin_send.at[number, k], "recv_sem": twin_recv.at[number, k]}
        go, come = (
            pltpu.make_async_remote_copy(
                src_ref=ref_at(me_core), dst_ref=ref_at(core), device_id=twin, device_id_type=MESH, **sems
            )
            for core in (me_core, 1 - me_core)
        )
        go.start()
        started.append((go, come))
        return (go, come)

    def arrive_and_pass_on(number, both, ref):
        passed = [pass_on(number, n_c - 1, lambda core: ref.at[core, me_p])]
        come_from = [slot_from for _, _, slot_from, _ in c_list]
        for at in reversed(range(len(both))):
            both[at][1].wait_recv()
            to, slot_from = c_list[at][0], come_from[at]
            passed.append(pass_on(number, at, lambda core: ref.at[core, slot_from]))
        for _, come in passed:
            come.wait_recv()

    def start_d(phase, s, r):
        both = start(d_list, depth_send.at[phase], depth_recv.at[phase], lambda t: s, r.at[me_d], lambda t: r.at[t])
        r[me_d] = s[...]
        return both

    slot = lax.broadcasted_iota(jnp.int32, (1, 1, LANE), 2) // SLOT

    def padded_t(ref):
        pad[:, :k_block, :] = ref[...].astype(F32)
        pad[:, k_block:, :] = jnp.zeros((i_q, SLOT - k_block, ch), F32)
        return pad[...].reshape(width, ch).T

    def pack(x):
        parts = [lanes(x, v).reshape(n_z, hz, LANE) for v in range(vl)]
        short = s5.shape[1] - vl * hz
        if short:
            parts.append(jnp.zeros((n_z, short, LANE), F32))
        return jnp.concatenate(parts, axis=1).astype(BF16)

    fetch[0].wait()
    x_hat, inv_std = norm_rows(padded_t(pair))
    normed = x_hat.astype(BF16)
    fetch[1].wait()
    w_in_t = w_in[...].astype(F32).T.astype(BF16)
    fetch[2].wait()
    lane_id = lax.broadcasted_iota(jnp.int32, (1, width), 1)
    row_mask = jnp.zeros((1, width), F32)
    for i in range(i_q):
        here = mask[me_r * i_block + me_d * i_q + i].astype(F32)
        row_mask = jnp.where(lane_id // SLOT == i, here, row_mask)
    col_mask = jnp.zeros((1, width), F32)
    for t in range(k_block):
        here = mask[me_c * k_block + t].astype(F32)
        col_mask = jnp.where(lane_id % SLOT == t, here, col_mask)
    pair_mask = row_mask * col_mask
    parts = []
    for block in range(2):
        both = dot(w_in_t[2 * block * hid : 2 * (block + 1) * hid], normed)
        sig, val = jax.nn.sigmoid(both[:hid]), both[hid:]
        proj[2 * block] = sig
        proj[2 * block + 1] = val
        parts.append((pair_mask * sig * val).reshape(n_z, hz, width))
    s1[...] = jnp.concatenate(parts, axis=1).astype(BF16)

    pl.semaphore_wait(barrier, len(peers))
    move = start_z(0, s1, r1)
    for f in fetch[3:]:
        f.wait()
    cot_t = padded_t(cot)
    gate_val = jax.nn.sigmoid(dot(w_gate[...].astype(F32).T.astype(BF16), normed))
    w_out_t = w_out[...].astype(F32).T.astype(BF16)
    arrive(move)

    x = r1[...].astype(F32)
    for v in range(vl):
        f1[v] = lanes(x, v).reshape(n_z * 2 * hz, LANE)
    for h in range(hz):
        for v in range(vl):
            a0, b0, a1, b1 = (
                f1[v, pl.ds(dd * half * 2 * hz + block * hz + h, half, stride=2 * hz), :]
                for dd in range(2) for block in range(2)
            )
            at = slice(v * LANE, (v + 1) * LANE)
            s2b[h, :, at] = jnp.concatenate([b0, b1], axis=0).astype(BF16)
            s2a[2 * h, :, at] = jnp.concatenate([a0, a1], axis=0).astype(BF16)
            s2a[2 * h + 1, :, at] = jnp.concatenate([a1, a0], axis=0).astype(BF16)

    def own_b():
        r2b[me_core, me_p] = s2b[me_p // 2]

    def own_a():
        r2a[me_core, me_p] = s2a[me_p]

    move = start_c(0, lambda t: s2b.at[t // 2], lambda t: r2b.at[me_core, t], own_b)
    move_a = start_c(1, lambda t: s2a.at[t], lambda t: r2a.at[me_core, t], own_a)
    arrive_and_pass_on(0, move, r2b)
    arrive(move_a)
    pass_a = pass_on(2, 0, lambda core: r2a.at[core])

    for core in range(2):
        x = r2b[core].astype(F32)
        for i, m in enumerate(to_matrix([lanes(x, v) for v in range(vl)], slot)):
            for dd in range(n_dd):
                at = ((core * n_dd + dd) * i_q + i) * half
                for g in range(groups):
                    bn[g, at : at + half, :] = lanes(m[dd * half : (dd + 1) * half], g)
    rows = []
    for core in range(2):
        for q in range(half):
            rows.append(jnp.concatenate(
                [bn[g, pl.ds(core * k_block * half + q, k_block, stride=half), :] for g in range(groups)], axis=-1
            ))
            rows.append(jnp.zeros((SLOT - k_block, full), F32))
    b_mat = jnp.concatenate(rows, axis=0).astype(BF16)
    x = r2a[me_core].astype(F32)[:, :half]
    a_own = jnp.concatenate(to_matrix([lanes(x, v) for v in range(vl)], slot), axis=0).astype(BF16)
    tri = lax.dot_general(a_own, b_mat, (((1,), (1,)), ((), ())), preferred_element_type=F32)
    for c, x in enumerate(from_matrix(tri.reshape(i_q, half, full), slot)):
        s3[c] = x.reshape(vl * half, LANE)
    size3 = vl * half

    def rows3(t):
        return pl.ds(pl.multiple_of(t * size3, size3), size3)

    def own_3():
        r3[rows3(me_p), :] = s3[me_p]

    move = start_c(2, lambda t: s3.at[t], lambda t: r3.at[rows3(t)], own_3)

    arrive([pass_a])
    rows = []
    for core in range(2):
        x = r2a[core].astype(F32)
        rows += to_matrix([lanes(x, v) for v in range(vl)], slot)
    a_mat = jnp.concatenate(rows, axis=0).astype(BF16)
    arrive(move)

    for dd in range(n_dd):
        for q in range(half):
            parts = [r3[pl.ds(dd * size3 + v * half + q, hz, stride=2 * size3), :] for v in range(vl)]
            short = s4.shape[1] - vl * hz
            if short:
                parts.append(jnp.zeros((short, LANE), F32))
            s4[dd * half + q] = jnp.concatenate(parts, axis=0).astype(BF16)
    move = start_z(1, s4, r4)
    arrive(move)

    x = r4[...].astype(F32)
    tri_t = jnp.concatenate([x[:, v * hz : (v + 1) * hz, :].reshape(hid, LANE) for v in range(vl)], axis=-1)
    y_hat, tri_std = norm_rows(tri_t)
    out_proj = dot(w_out_t, y_hat.astype(BF16))
    d_o = (cot_t * gate_val).astype(BF16)
    d_y = dot(w_out[...], d_o)
    s5[...] = pack(norm_back(y_hat, tri_std, d_y))
    move = start_z(2, s5, r5)

    def natural(x):
        return x.T.reshape(i_q, SLOT, ch)[:, :k_block, :].reshape(i_q * k_block, ch).astype(BF16)

    su[...] = natural(gate_val * out_proj)
    d_gate_pre = (cot_t * out_proj * gate_val * (1.0 - gate_val)).astype(BF16)
    d_gate = dot(w_gate[...], d_gate_pre)
    arrive(move)
    update_move = start_d(0, su, ru)

    pitch = s5.shape[1]
    f5[...] = r5[...].astype(F32).reshape(n_z * pitch, LANE)
    for h in range(hz):
        for v in range(vl):
            t0, t1 = (f5[pl.ds(dd * half * pitch + v * hz + h, half, stride=pitch), :] for dd in range(2))
            at = slice(v * LANE, (v + 1) * LANE)
            s6[2 * h, :, at] = jnp.concatenate([t0, t1], axis=0).astype(BF16)
            s6[2 * h + 1, :, at] = jnp.concatenate([t1, t0], axis=0).astype(BF16)

    def own_6():
        r6[me_core, me_p] = s6[me_p]

    move = start_c(3, lambda t: s6.at[t], lambda t: r6.at[me_core, t], own_6)
    arrive_and_pass_on(1, move, r6)
    for core in range(2):
        x = r6[core].astype(F32)
        for i, m in enumerate(to_matrix([lanes(x, v) for v in range(vl)], slot)):
            tgf[core, i] = m
    tg_own = tgf[me_core, :, :half, :].reshape(i_q * half, full).astype(BF16)
    mine = pl.ds(pl.multiple_of(me_core * (full // 2), full // 2), full // 2)
    tg_t = tgf[:, :, :, mine].reshape(2 * i_q * 2 * half, full // 2).T.astype(BF16)
    part_b = dot(tg_t, a_mat)
    for g in range(groups):
        gf[g] = lanes(part_b, g)
    grad_a = dot(tg_own, b_mat).reshape(i_q, half, full)
    rows = []
    for i in range(i_q):
        rows.append(grad_a[i])
        rows.append(jnp.concatenate(
            [gf[g, pl.ds(me_dd * i_q + i, half, stride=SLOT), :] for g in range(groups)], axis=-1
        ))
    both = jnp.concatenate(rows, axis=0).reshape(i_q, 2 * half, full)
    for c, x in enumerate(from_matrix(both, slot)):
        for v in range(vl):
            s8[c, :, v * LANE : (v + 1) * LANE] = x[v].astype(BF16)

    def own_8():
        r8[me_p] = s8[me_p]

    move = start_c(4, lambda t: s8.at[t], lambda t: r8.at[t], own_8)
    arrive(move)
    x = r8[...].astype(F32)
    for v in range(vl):
        f8[v] = lanes(x, v).reshape(n_c * 2 * half, LANE)
    for dd in range(n_dd):
        for q in range(half):
            for v in range(vl):
                s9[dd * half + q, :, v * LANE : (v + 1) * LANE] = jnp.concatenate(
                    [
                        f8[v, pl.ds((dd * 2 + block) * half + q, hz, stride=4 * half), :]
                        for block in range(2)
                    ],
                    axis=0,
                ).astype(BF16)
    move = start_z(3, s9, r9)
    arrive(move)

    d_normed = d_gate
    x = r9[...].astype(F32)
    for block in range(2):
        grad = x[:, block * hz : (block + 1) * hz, :].reshape(hid, width) * pair_mask
        sig, val = proj[2 * block], proj[2 * block + 1]
        d_pre = (grad * val * sig * (1.0 - sig)).astype(BF16)
        d_val = (grad * sig).astype(BF16)
        d_normed = d_normed + dot(w_in[:, 2 * block * hid : (2 * block + 1) * hid], d_pre)
        d_normed = d_normed + dot(w_in[:, (2 * block + 1) * hid : (2 * block + 2) * hid], d_val)
    sg[...] = natural(norm_back(x_hat, inv_std, d_normed))
    move = start_d(1, sg, rg)
    arrive(update_move)
    for d in range(n_d):
        update_out[d * i_q : (d + 1) * i_q] = ru[d].astype(F32).reshape(i_q, k_block, ch).astype(BF16)
    arrive(move)
    for d in range(n_d):
        grad_out[d * i_q : (d + 1) * i_q] = rg[d].astype(F32).reshape(i_q, k_block, ch).astype(BF16)
    for go, _ in started:
        go.wait_send()


def shards(sizes, pair, cotangent, w_in, w_gate, w_out, residue_mask):
    n_d, n_r, n_c = sizes
    n_x = 4 if n_c == 16 else 2
    i_block, k_block, ch = pair.shape
    hid = w_out.shape[0]
    i_q = i_block // n_d
    width = i_q * SLOT
    vl = width // LANE
    n_z = (n_r // 2) * n_d
    half = n_r
    hz = hid // n_z
    full = n_c * SLOT
    groups = max(full // LANE, 1)
    pitch = -(-vl * hz // 16) * 16
    vm = pltpu.VMEM
    scratch = [
        pltpu.SMEM(residue_mask.shape, jnp.int32),
        vm((i_q, k_block, ch), BF16),
        vm((i_q, k_block, ch), BF16),
        vm(w_in.shape, BF16),
        vm(w_gate.shape, BF16),
        vm(w_out.shape, BF16),
        pltpu.SemaphoreType.DMA((6,)),
        vm((i_q, SLOT, ch), F32),
        vm((4, hid, width), F32),
        vm((n_z, 2 * hz, width), BF16),
        vm((n_z, 2 * hz, width), BF16),
        vm((vl, n_z * 2 * hz, LANE), F32),
        vm((n_c, 2 * half, width), BF16),
        vm((n_c // 2, 2 * half, width), BF16),
        vm((2, n_c, 2 * half, width), BF16),
        vm((2, n_c, 2 * half, width), BF16),
        vm((groups, 2 * k_block * half, LANE), F32),
        vm((n_c, vl * half, LANE), F32),
        vm((n_c * vl * half, LANE), F32),
        vm((n_z, pitch, LANE), BF16),
        vm((n_z, pitch, LANE), BF16),
        vm((n_z, pitch, LANE), BF16),
        vm((n_z, pitch, LANE), BF16),
        vm((n_z * pitch, LANE), F32),
        vm((n_c, 2 * half, width), BF16),
        vm((2, n_c, 2 * half, width), BF16),
        vm((2, i_q, 2 * half, full), F32),
        vm((groups, full // 2, LANE), F32),
        vm((n_c, 2 * half, width), BF16),
        vm((n_c, 2 * half, width), BF16),
        vm((vl, n_c * 2 * half, LANE), F32),
        vm((n_z, 2 * hz, width), BF16),
        vm((n_z, 2 * hz, width), BF16),
        vm((i_q * k_block, ch), BF16),
        vm((n_d, i_q * k_block, ch), BF16),
        vm((i_q * k_block, ch), BF16),
        vm((n_d, i_q * k_block, ch), BF16),
    ]
    for phases, size in ((4, n_z), (5, n_c), (2, n_d), (3, n_c)):
        scratch += [pltpu.SemaphoreType.DMA((phases, size))] * 2
    whole = pl.BlockSpec(memory_space=pltpu.VMEM)
    return pl.pallas_call(
        functools.partial(kernel, (n_d, n_r, n_c, n_x, i_block, k_block, ch, hid)),
        out_shape=(jax.ShapeDtypeStruct(pair.shape, BF16),) * 2,
        in_specs=[pl.BlockSpec(memory_space=pl.ANY)] * 6,
        out_specs=(whole, whole),
        scratch_shapes=scratch,
        compiler_params=pltpu.CompilerParams(
            collective_id=0, has_side_effects=True, vmem_limit_bytes=60 * 1024 * 1024
        ),
    )(residue_mask, pair, cotangent, w_in, w_gate, w_out)


def solution(mesh):
    in_specs = (P("row", "col", None), P("row", "col", None), P(), P(), P(), P())
    out_specs = (P("row", "col", None), P("row", "col", None))
    sizes = (mesh.shape["depth"], mesh.shape["row"], mesh.shape["col"])
    return jax.shard_map(
        functools.partial(shards, sizes), mesh=mesh, in_specs=in_specs, out_specs=out_specs, check_vma=False
    )
```

```python
import functools

import jax
import jax.numpy as jnp
from jax import lax
from jax.experimental import pallas as pl
from jax.experimental.pallas import tpu as pltpu
from jax.sharding import PartitionSpec as P

MESH = pl.DeviceIdType.MESH
F32 = jnp.float32
BF16 = jnp.bfloat16
SLOT = 32
LANE = 128
PER = LANE // SLOT


def dot(left, right):
    return jnp.dot(left, right, preferred_element_type=F32)


def norm_rows(values):
    average = jnp.mean(values, axis=0, keepdims=True)
    centered = values - average
    variance = jnp.mean(centered * centered, axis=0, keepdims=True)
    inv_std = lax.rsqrt(variance + 1e-05)
    return (centered * inv_std, inv_std)


def norm_back(x_hat, inv_std, upstream):
    first = jnp.mean(upstream, axis=0, keepdims=True)
    second = jnp.mean(upstream * x_hat, axis=0, keepdims=True)
    return inv_std * (upstream - first - x_hat * second)


def lanes(x, v):
    return x[..., v * LANE : (v + 1) * LANE]


def to_matrix(tiles, slot):
    out = []
    for x in tiles:
        groups, rows = x.shape[0] // PER, x.shape[1]
        x = x.reshape(groups, PER, rows, LANE)
        for s in range(PER):
            acc = None
            for c in range(PER):
                y = x[:, c]
                if c != s:
                    y = pltpu.roll(y, (SLOT * (c - s)) % LANE, 2)
                acc = y if acc is None else jnp.where(slot == c, y, acc)
            out.append(jnp.concatenate([acc[g] for g in range(groups)], axis=-1))
    return out


def from_matrix(matrix, slot):
    count, rows, width = matrix.shape
    x = matrix.reshape(count // PER, PER, rows, width)
    out = []
    for g in range(width // LANE):
        part = lanes(x, g)
        for c in range(PER):
            acc = None
            for s in range(PER):
                y = part[:, s]
                if c != s:
                    y = pltpu.roll(y, (SLOT * (s - c)) % LANE, 2)
                acc = y if acc is None else jnp.where(slot == s, y, acc)
            out.append(acc)
    return out


def kernel(
    dims,
    mask_hbm, pair_hbm, cot_hbm, w_in_hbm, w_gate_hbm, w_out_hbm,
    update_out, grad_out,
    mask, pair, cot, w_in, w_gate, w_out, in_sem,
    pad, proj, s1, r1, f1, s2, r2, t2, bn, all_a, s3, r3, s4, r4, s5, r5, f5, s6, r6, t6, tgf,
    gf, s8, r8, f8, s9, r9, su, ru, sg, rg,
    z_send, z_recv, col_send, col_recv, depth_send, depth_recv, twin_send, twin_recv,
):
    n_d, n_r, n_c, n_x, i_block, k_block, ch, hid = dims
    n_zh, n_dd, n_y = n_r // 2, n_d // 2, n_c // n_x
    n_z = n_zh * n_d
    hz = hid // n_z
    i_q = i_block // n_d
    width = i_q * SLOT
    vl = width // LANE
    half = 2 * n_zh
    full = n_c * SLOT
    groups = full // LANE
    me_d, me_r, me_c = lax.axis_index("depth"), lax.axis_index("row"), lax.axis_index("col")
    me_zh, me_core = me_r // 2, me_r % 2

    def z_slot(zh, d):
        return (d % n_dd) * half + (d // n_dd) * n_zh + zh

    def c_slot(c):
        return ((c // 2) % 2) * half + (c % 2) * n_zh + c // 4

    me_s, me_p = z_slot(me_zh, me_d), c_slot(me_c)
    me_dd = me_p % 2

    def z_peer(o):
        z = lax.rem(me_zh * n_d + me_d + o + n_z, n_z)
        zh, d = z // n_d, z % n_d
        return {"row": zh * 2 + me_core, "depth": d}, z_slot(zh, d)

    def c_peer(ox, oy):
        x = lax.rem(me_c // n_y + ox + n_x, n_x)
        y = lax.rem(me_c % n_y + oy + n_y, n_y)
        c = x * n_y + y
        return {"col": c}, c_slot(c)

    def d_peer(o):
        d = lax.rem(me_d + o + n_d, n_d)
        return {"depth": d}, d

    z_offsets = sorted(range(1, n_z), key=lambda o: -min(o, n_z - o))
    c_offsets = sorted(
        [(x, y) for x in range(n_x) for y in range(n_y)],
        key=lambda o: -(min(o[0], n_x - o[0]) + min(o[1], n_y - o[1])),
    )
    d_offsets = list(range(1, n_d))

    z_list = [z_peer(o) + (z_peer(-o)[1], k) for k, o in enumerate(z_offsets)]
    d_list = [d_peer(o) + (d_peer(-o)[1], k) for k, o in enumerate(d_offsets)]
    c_list = [
        c_peer(ox, oy) + (c_peer(-ox, -oy)[1], k) for k, (ox, oy) in enumerate(c_offsets) if (ox, oy) != (0, 0)
    ]
    twin = {"row": me_zh * 2 + 1 - me_core}

    barrier = pltpu.get_barrier_semaphore()
    peers = [to for to, _, _, _ in z_list + c_list] + [twin]
    for to in peers:
        pl.semaphore_signal(barrier, inc=1, device_id=to, device_id_type=MESH)

    own_rows = pl.ds(me_d * i_q, i_q)
    fetch = [
        pltpu.make_async_copy(a, b, in_sem.at[k])
        for k, (a, b) in enumerate([
            (pair_hbm.at[own_rows], pair), (w_in_hbm, w_in), (mask_hbm, mask),
            (cot_hbm.at[own_rows], cot), (w_gate_hbm, w_gate), (w_out_hbm, w_out),
        ])
    ]
    for f in fetch:
        f.start()

    started = []

    def start(peer_list, send, recv, src_at, dst_mine, dst_from):
        both = []
        for to, slot_to, slot_from, k in peer_list:
            go = pltpu.make_async_remote_copy(
                src_ref=src_at(slot_to), dst_ref=dst_mine, send_sem=send.at[k], recv_sem=recv.at[k],
                device_id=to, device_id_type=MESH,
            )
            come = pltpu.make_async_remote_copy(
                src_ref=src_at(slot_to), dst_ref=dst_from(slot_from), send_sem=send.at[k], recv_sem=recv.at[k],
                device_id=to, device_id_type=MESH,
            )
            go.start()
            both.append((go, come))
        started.extend(both)
        return both

    def arrive(both):
        for _, come in both:
            come.wait_recv()

    def start_z(phase, s, r):
        sems = (z_send.at[phase], z_recv.at[phase])
        both = start(z_list[:9], *sems, lambda t: s.at[t], r.at[me_s], lambda t: r.at[t])
        for pair_ in both:
            pair_[0].wait_send()
        del started[-9:]
        both = both + start(z_list[9:], *sems, lambda t: s.at[t], r.at[me_s], lambda t: r.at[t])
        r[me_s] = s[me_s]
        return both

    def start_c(phase, src_at, dst_at, own):
        both = start(c_list, col_send.at[phase], col_recv.at[phase], src_at, dst_at(me_p), dst_at)
        own()
        return both

    def pass_on(k, src, dst):
        go = pltpu.make_async_remote_copy(
            src_ref=src, dst_ref=dst, send_sem=twin_send.at[k], recv_sem=twin_recv.at[k],
            device_id=twin, device_id_type=MESH,
        )
        go.start()
        started.append((go, go))
        return started[-1:]

    def start_d(phase, s, r):
        both = start(d_list, depth_send.at[phase], depth_recv.at[phase], lambda t: s, r.at[me_d], lambda t: r.at[t])
        r[me_d] = s[...]
        return both

    slot = lax.broadcasted_iota(jnp.int32, (1, 1, LANE), 2) // SLOT

    def padded_t(ref):
        pad[:, :k_block, :] = ref[...].astype(F32)
        pad[:, k_block:, :] = jnp.zeros((i_q, SLOT - k_block, ch), F32)
        return pad[...].reshape(width, ch).T

    def pack(x):
        return jnp.stack([lanes(x, v).reshape(n_z, hz, LANE) for v in range(vl)], axis=1).astype(BF16)

    fetch[0].wait()
    x_hat, inv_std = norm_rows(padded_t(pair))
    normed = x_hat.astype(BF16)
    fetch[1].wait()
    w_in_t = w_in[...].astype(F32).T.astype(BF16)
    fetch[2].wait()
    lane_id = lax.broadcasted_iota(jnp.int32, (1, width), 1)
    row_mask = jnp.zeros((1, width), F32)
    for i in range(i_q):
        here = mask[me_r * i_block + me_d * i_q + i].astype(F32)
        row_mask = jnp.where(lane_id // SLOT == i, here, row_mask)
    col_mask = jnp.zeros((1, width), F32)
    for t in range(k_block):
        here = mask[me_c * k_block + t].astype(F32)
        col_mask = jnp.where(lane_id % SLOT == t, here, col_mask)
    pair_mask = row_mask * col_mask
    parts = []
    for block in range(2):
        both = dot(w_in_t[2 * block * hid : 2 * (block + 1) * hid], normed)
        sig, val = jax.nn.sigmoid(both[:hid]), both[hid:]
        proj[2 * block] = sig
        proj[2 * block + 1] = val
        parts.append((pair_mask * sig * val).reshape(n_z, hz, width))
    s1[...] = jnp.concatenate(parts, axis=1).astype(BF16)

    pl.semaphore_wait(barrier, len(peers))
    move = start_z(0, s1, r1)
    for f in fetch[3:]:
        f.wait()
    cot_t = padded_t(cot)
    gate_val = jax.nn.sigmoid(dot(w_gate[...].astype(F32).T.astype(BF16), normed))
    w_out_t = w_out[...].astype(F32).T.astype(BF16)
    arrive(move)

    x = r1[...].astype(F32)
    for v in range(vl):
        f1[v] = lanes(x, v).reshape(n_z * 2 * hz, LANE)
    for h in range(hz):
        for v in range(vl):
            a0, b0, a1, b1 = (
                f1[v, pl.ds(dd * half * 2 * hz + block * hz + h, half, stride=2 * hz), :]
                for dd in range(2) for block in range(2)
            )
            at = slice(v * LANE, (v + 1) * LANE)
            s2[2 * h, :, at] = jnp.concatenate([b0, b1, a0, a1], axis=0).astype(BF16)
            s2[2 * h + 1, :, at] = jnp.concatenate([b0, b1, a1, a0], axis=0).astype(BF16)

    def own_2():
        r2[me_p] = s2[me_p]

    b_part, a_part = slice(0, 2 * half), slice(2 * half, 4 * half)
    move = start_c(0, lambda t: s2.at[t], lambda t: r2.at[t], own_2)
    arrive(move)
    pass_b = pass_on(0, r2.at[:, b_part], t2.at[:, b_part])
    pass_a = pass_on(1, r2.at[:, a_part], t2.at[:, a_part])
    x = r2[:, a_part, :].astype(F32)
    a_rows = to_matrix([lanes(x, v) for v in range(vl)], slot)
    a_own = jnp.concatenate([m[:half] for m in a_rows], axis=0).astype(BF16)

    def place_b(core, ref):
        x = ref[:, b_part, :].astype(F32)
        for i, m in enumerate(to_matrix([lanes(x, v) for v in range(vl)], slot)):
            for dd in range(n_dd):
                at = (dd * i_q + i) * half
                for g in range(groups):
                    bn[g, core, at : at + half, :] = lanes(m[dd * half : (dd + 1) * half], g)

    place_b(me_core, r2)
    arrive(pass_b)
    place_b(1 - me_core, t2)
    rows = []
    for core in range(2):
        for q in range(half):
            rows.append(jnp.concatenate(
                [bn[g, core, pl.ds(q, k_block, stride=half), :] for g in range(groups)], axis=-1
            ))
            rows.append(jnp.zeros((SLOT - k_block, full), F32))
    b_mat = jnp.concatenate(rows, axis=0).astype(BF16)
    tri = lax.dot_general(a_own, b_mat, (((1,), (1,)), ((), ())), preferred_element_type=F32)
    for c, x in enumerate(from_matrix(tri.reshape(i_q, half, full), slot)):
        s3[c] = x.reshape(vl * half, LANE)
    size3 = vl * half

    def rows3(t):
        return pl.ds(pl.multiple_of(t * size3, size3), size3)

    def own_3():
        r3[rows3(me_p), :] = s3[me_p]

    move = start_c(2, lambda t: s3.at[t], lambda t: r3.at[rows3(t)], own_3)

    all_a[me_core] = jnp.concatenate(a_rows, axis=0).astype(BF16)
    arrive(pass_a)
    x = t2[:, a_part, :].astype(F32)
    all_a[1 - me_core] = jnp.concatenate(to_matrix([lanes(x, v) for v in range(vl)], slot), axis=0).astype(BF16)
    arrive(move)

    for dd in range(n_dd):
        for q in range(half):
            parts = [r3[pl.ds(dd * size3 + v * half + q, hz, stride=2 * size3), :] for v in range(vl)]
            s4[dd * half + q] = jnp.stack(parts, axis=0).astype(BF16)
    move = start_z(1, s4, r4)
    arrive(move)

    x = r4[...].astype(F32)
    tri_t = jnp.concatenate([x[:, v].reshape(hid, LANE) for v in range(vl)], axis=-1)
    y_hat, tri_std = norm_rows(tri_t)
    out_proj = dot(w_out_t, y_hat.astype(BF16))
    d_o = (cot_t * gate_val).astype(BF16)
    d_y = dot(w_out[...], d_o)
    s5[...] = pack(norm_back(y_hat, tri_std, d_y))
    move = start_z(2, s5, r5)

    def natural(x):
        return x.T.reshape(i_q, SLOT, ch)[:, :k_block, :].reshape(i_q * k_block, ch).astype(BF16)

    su[...] = natural(gate_val * out_proj)
    d_gate_pre = (cot_t * out_proj * gate_val * (1.0 - gate_val)).astype(BF16)
    d_gate = dot(w_gate[...], d_gate_pre)
    arrive(move)
    update_move = start_d(0, su, ru)

    pitch = vl * hz
    f5[...] = r5[...].astype(F32).reshape(n_z * pitch, LANE)
    for h in range(hz):
        for v in range(vl):
            t0, t1 = (f5[pl.ds(dd * half * pitch + v * hz + h, half, stride=pitch), :] for dd in range(2))
            at = slice(v * LANE, (v + 1) * LANE)
            s6[2 * h, :, at] = jnp.concatenate([t0, t1], axis=0).astype(BF16)
            s6[2 * h + 1, :, at] = jnp.concatenate([t1, t0], axis=0).astype(BF16)

    def own_6():
        r6[me_p] = s6[me_p]

    move = start_c(3, lambda t: s6.at[t], lambda t: r6.at[t], own_6)
    arrive(move)
    pass_t = pass_on(2, r6, t6)
    x = r6[...].astype(F32)
    rows = to_matrix([lanes(x, v) for v in range(vl)], slot)
    for i, m in enumerate(rows):
        tgf[me_core, i] = m
    tg_own = jnp.concatenate([m[:half] for m in rows], axis=0).astype(BF16)
    grad_a = dot(tg_own, b_mat).reshape(i_q, half, full)
    arrive(pass_t)
    x = t6[...].astype(F32)
    for i, m in enumerate(to_matrix([lanes(x, v) for v in range(vl)], slot)):
        tgf[1 - me_core, i] = m
    mine = pl.ds(pl.multiple_of(me_core * (full // 2), full // 2), full // 2)
    tg_t = tgf[:, :, :, mine].reshape(2 * i_q * 2 * half, full // 2).T.astype(BF16)
    part_b = dot(tg_t, all_a[...].reshape(2 * i_q * 2 * half, full))
    for g in range(groups):
        gf[g] = lanes(part_b, g)
    rows = []
    for i in range(i_q):
        rows.append(grad_a[i])
        rows.append(jnp.concatenate(
            [gf[g, pl.ds(me_dd * i_q + i, half, stride=SLOT), :] for g in range(groups)], axis=-1
        ))
    both = jnp.concatenate(rows, axis=0).reshape(i_q, 2 * half, full)
    for c, x in enumerate(from_matrix(both, slot)):
        for v in range(vl):
            s8[c, :, v * LANE : (v + 1) * LANE] = x[v].astype(BF16)

    def own_8():
        r8[me_p] = s8[me_p]

    move = start_c(4, lambda t: s8.at[t], lambda t: r8.at[t], own_8)
    arrive(move)
    x = r8[...].astype(F32)
    for v in range(vl):
        f8[v] = lanes(x, v).reshape(n_c * 2 * half, LANE)
    for dd in range(n_dd):
        for q in range(half):
            for v in range(vl):
                s9[dd * half + q, :, v * LANE : (v + 1) * LANE] = jnp.concatenate(
                    [
                        f8[v, pl.ds((dd * 2 + block) * half + q, hz, stride=4 * half), :]
                        for block in range(2)
                    ],
                    axis=0,
                ).astype(BF16)
    move = start_z(3, s9, r9)
    arrive(move)

    d_normed = d_gate
    x = r9[...].astype(F32)
    for block in range(2):
        grad = x[:, block * hz : (block + 1) * hz, :].reshape(hid, width) * pair_mask
        sig, val = proj[2 * block], proj[2 * block + 1]
        d_pre = (grad * val * sig * (1.0 - sig)).astype(BF16)
        d_val = (grad * sig).astype(BF16)
        d_normed = d_normed + dot(w_in[:, 2 * block * hid : (2 * block + 1) * hid], d_pre)
        d_normed = d_normed + dot(w_in[:, (2 * block + 1) * hid : (2 * block + 2) * hid], d_val)
    sg[...] = natural(norm_back(x_hat, inv_std, d_normed))
    move = start_d(1, sg, rg)
    arrive(update_move)
    for d in range(n_d):
        update_out[d * i_q : (d + 1) * i_q] = ru[d].astype(F32).reshape(i_q, k_block, ch).astype(BF16)
    arrive(move)
    for d in range(n_d):
        grad_out[d * i_q : (d + 1) * i_q] = rg[d].astype(F32).reshape(i_q, k_block, ch).astype(BF16)
    for go, _ in started:
        go.wait_send()


def shards(sizes, pair, cotangent, w_in, w_gate, w_out, residue_mask):
    n_d, n_r, n_c = sizes
    n_x = 4 if n_c == 16 else 2
    i_block, k_block, ch = pair.shape
    hid = w_out.shape[0]
    i_q = i_block // n_d
    width = i_q * SLOT
    vl = width // LANE
    n_z = (n_r // 2) * n_d
    half = n_r
    hz = hid // n_z
    full = n_c * SLOT
    groups = max(full // LANE, 1)
    pitch = vl * hz
    vm = pltpu.VMEM
    scratch = [
        pltpu.SMEM(residue_mask.shape, jnp.int32),
        vm((i_q, k_block, ch), BF16),
        vm((i_q, k_block, ch), BF16),
        vm(w_in.shape, BF16),
        vm(w_gate.shape, BF16),
        vm(w_out.shape, BF16),
        pltpu.SemaphoreType.DMA((6,)),
        vm((i_q, SLOT, ch), F32),
        vm((4, hid, width), F32),
        vm((n_z, 2 * hz, width), BF16),
        vm((n_z, 2 * hz, width), BF16),
        vm((vl, n_z * 2 * hz, LANE), F32),
        vm((n_c, 4 * half, width), BF16),
        vm((n_c, 4 * half, width), BF16),
        vm((n_c, 4 * half, width), BF16),
        vm((groups, 2, k_block * half, LANE), F32),
        vm((2, i_q * 2 * half, full), BF16),
        vm((n_c, vl * half, LANE), F32),
        vm((n_c * vl * half, LANE), F32),
        vm((n_z, vl, hz, LANE), BF16),
        vm((n_z, vl, hz, LANE), BF16),
        vm((n_z, vl, hz, LANE), BF16),
        vm((n_z, vl, hz, LANE), BF16),
        vm((n_z * pitch, LANE), F32),
        vm((n_c, 2 * half, width), BF16),
        vm((n_c, 2 * half, width), BF16),
        vm((n_c, 2 * half, width), BF16),
        vm((2, i_q, 2 * half, full), F32),
        vm((groups, full // 2, LANE), F32),
        vm((n_c, 2 * half, width), BF16),
        vm((n_c, 2 * half, width), BF16),
        vm((vl, n_c * 2 * half, LANE), F32),
        vm((n_z, 2 * hz, width), BF16),
        vm((n_z, 2 * hz, width), BF16),
        vm((i_q * k_block, ch), BF16),
        vm((n_d, i_q * k_block, ch), BF16),
        vm((i_q * k_block, ch), BF16),
        vm((n_d, i_q * k_block, ch), BF16),
    ]
    for phases, size in ((4, n_z), (5, n_c), (2, n_d)):
        scratch += [pltpu.SemaphoreType.DMA((phases, size))] * 2
    scratch += [pltpu.SemaphoreType.DMA((3,))] * 2
    whole = pl.BlockSpec(memory_space=pltpu.VMEM)
    return pl.pallas_call(
        functools.partial(kernel, (n_d, n_r, n_c, n_x, i_block, k_block, ch, hid)),
        out_shape=(jax.ShapeDtypeStruct(pair.shape, BF16),) * 2,
        in_specs=[pl.BlockSpec(memory_space=pl.ANY)] * 6,
        out_specs=(whole, whole),
        scratch_shapes=scratch,
        compiler_params=pltpu.CompilerParams(
            collective_id=0, has_side_effects=True, vmem_limit_bytes=60 * 1024 * 1024
        ),
    )(residue_mask, pair, cotangent, w_in, w_gate, w_out)


def solution(mesh):
    in_specs = (P("row", "col", None), P("row", "col", None), P(), P(), P(), P())
    out_specs = (P("row", "col", None), P("row", "col", None))
    sizes = (mesh.shape["depth"], mesh.shape["row"], mesh.shape["col"])
    return jax.shard_map(
        functools.partial(shards, sizes), mesh=mesh, in_specs=in_specs, out_specs=out_specs, check_vma=False
    )
```

```python
import functools

import jax
import jax.numpy as jnp
from jax import lax
from jax.experimental import pallas as pl
from jax.experimental.pallas import tpu as pltpu
from jax.sharding import PartitionSpec as P

MESH = pl.DeviceIdType.MESH
F32 = jnp.float32
BF16 = jnp.bfloat16
SLOT = 32
LANE = 128
PER = LANE // SLOT
PAD_LANES = 8


def dot(left, right):
    return jnp.dot(left, right, preferred_element_type=F32)


def norm_rows(values):
    average = jnp.mean(values, axis=0, keepdims=True)
    centered = values - average
    variance = jnp.mean(centered * centered, axis=0, keepdims=True)
    inv_std = lax.rsqrt(variance + 1e-05)
    return (centered * inv_std, inv_std)


def norm_back(x_hat, inv_std, upstream):
    first = jnp.mean(upstream, axis=0, keepdims=True)
    second = jnp.mean(upstream * x_hat, axis=0, keepdims=True)
    return inv_std * (upstream - first - x_hat * second)


def lanes(x, v):
    return x[..., v * LANE : (v + 1) * LANE]


def to_matrix(tiles, slot):
    out = []
    for x in tiles:
        groups, rows = x.shape[0] // PER, x.shape[1]
        x = x.reshape(groups, PER, rows, LANE)
        for s in range(PER):
            acc = None
            for c in range(PER):
                y = x[:, c]
                if c != s:
                    y = pltpu.roll(y, (SLOT * (c - s)) % LANE, 2)
                acc = y if acc is None else jnp.where(slot == c, y, acc)
            out.append(jnp.concatenate([acc[g] for g in range(groups)], axis=-1))
    return out


def fold(a, b, chunk):
    last, per_slot = b[-1], SLOT // PAD_LANES
    out = []
    for j, tile in enumerate(a):
        moved = pltpu.roll(last, PAD_LANES * (per_slot - 1 - j), last.ndim - 1)
        out.append(jnp.where(chunk == per_slot - 1, moved, tile))
    return out + b[:-1]


def unfold(tiles, chunk):
    per_slot = SLOT // PAD_LANES
    last = jnp.zeros_like(tiles[0])
    a = []
    for j, tile in enumerate(tiles[: per_slot - 1]):
        moved = pltpu.roll(tile, LANE - PAD_LANES * (per_slot - 1 - j), tile.ndim - 1)
        last = jnp.where(chunk == j, moved, last)
        a.append(jnp.where(chunk == per_slot - 1, 0.0, tile))
    return a, tiles[per_slot - 1 :] + [last]


def from_matrix(matrix, slot):
    count, rows, width = matrix.shape
    x = matrix.reshape(count // PER, PER, rows, width)
    out = []
    for g in range(width // LANE):
        part = lanes(x, g)
        for c in range(PER):
            acc = None
            for s in range(PER):
                y = part[:, s]
                if c != s:
                    y = pltpu.roll(y, (SLOT * (s - c)) % LANE, 2)
                acc = y if acc is None else jnp.where(slot == s, y, acc)
            out.append(acc)
    return out


def kernel(
    dims,
    mask_hbm, pair_hbm, cot_hbm, w_in_hbm, w_gate_hbm, w_out_hbm,
    update_out, grad_out,
    mask, pair, cot, w_in, w_gate, w_out, in_sem,
    pad, proj, s1, r1, f1, s2, r2, t2, bn, all_a, s3, r3, s4, r4, s5, r5, f5, s6, r6, t6, tgf,
    gf, s8, r8, f8, s9, r9, su, ru, sg, rg,
    z_send, z_recv, col_send, col_recv, depth_send, depth_recv, twin_send, twin_recv,
):
    n_d, n_r, n_c, n_x, i_block, k_block, ch, hid = dims
    n_zh, n_dd, n_y = n_r // 2, n_d // 2, n_c // n_x
    n_z = n_zh * n_d
    hz = hid // n_z
    i_q = i_block // n_d
    width = i_q * SLOT
    vl = width // LANE
    half = 2 * n_zh
    full = n_c * SLOT
    groups = full // LANE
    me_d, me_r, me_c = lax.axis_index("depth"), lax.axis_index("row"), lax.axis_index("col")
    me_zh, me_core = me_r // 2, me_r % 2

    def z_slot(zh, d):
        return (d % n_dd) * half + (d // n_dd) * n_zh + zh

    def c_slot(c):
        return ((c // 2) % 2) * half + (c % 2) * n_zh + c // 4

    me_s, me_p = z_slot(me_zh, me_d), c_slot(me_c)
    me_dd = me_p % 2

    def z_peer(o):
        z = lax.rem(me_zh * n_d + me_d + o + n_z, n_z)
        zh, d = z // n_d, z % n_d
        return {"row": zh * 2 + me_core, "depth": d}, z_slot(zh, d)

    def c_peer(ox, oy):
        x = lax.rem(me_c // n_y + ox + n_x, n_x)
        y = lax.rem(me_c % n_y + oy + n_y, n_y)
        c = x * n_y + y
        return {"col": c}, c_slot(c)

    def d_peer(o):
        d = lax.rem(me_d + o + n_d, n_d)
        return {"depth": d}, d

    z_offsets = sorted(range(1, n_z), key=lambda o: -min(o, n_z - o))
    c_offsets = sorted(
        [(x, y) for x in range(n_x) for y in range(n_y)],
        key=lambda o: -(min(o[0], n_x - o[0]) + min(o[1], n_y - o[1])),
    )
    d_offsets = list(range(1, n_d))

    z_list = [z_peer(o) + (z_peer(-o)[1], k) for k, o in enumerate(z_offsets)]
    d_list = [d_peer(o) + (d_peer(-o)[1], k) for k, o in enumerate(d_offsets)]
    c_list = [
        c_peer(ox, oy) + (c_peer(-ox, -oy)[1], k) for k, (ox, oy) in enumerate(c_offsets) if (ox, oy) != (0, 0)
    ]
    twin = {"row": me_zh * 2 + 1 - me_core}

    barrier = pltpu.get_barrier_semaphore()
    peers = [to for to, _, _, _ in z_list + c_list] + [twin]
    for to in peers:
        pl.semaphore_signal(barrier, inc=1, device_id=to, device_id_type=MESH)

    own_rows = pl.ds(me_d * i_q, i_q)
    fetch = [
        pltpu.make_async_copy(a, b, in_sem.at[k])
        for k, (a, b) in enumerate([
            (pair_hbm.at[own_rows], pair), (w_in_hbm, w_in), (mask_hbm, mask),
            (cot_hbm.at[own_rows], cot), (w_gate_hbm, w_gate), (w_out_hbm, w_out),
        ])
    ]
    for f in fetch:
        f.start()

    started = []

    def start(peer_list, send, recv, src_at, dst_mine, dst_from):
        both = []
        for to, slot_to, slot_from, k in peer_list:
            go = pltpu.make_async_remote_copy(
                src_ref=src_at(slot_to), dst_ref=dst_mine, send_sem=send.at[k], recv_sem=recv.at[k],
                device_id=to, device_id_type=MESH,
            )
            come = pltpu.make_async_remote_copy(
                src_ref=src_at(slot_to), dst_ref=dst_from(slot_from), send_sem=send.at[k], recv_sem=recv.at[k],
                device_id=to, device_id_type=MESH,
            )
            go.start()
            both.append((go, come))
        started.extend(both)
        return both

    def arrive(both):
        for _, come in both:
            come.wait_recv()

    def start_z(phase, s, r):
        sems = (z_send.at[phase], z_recv.at[phase])
        both = start(z_list[:9], *sems, lambda t: s.at[t], r.at[me_s], lambda t: r.at[t])
        for pair_ in both:
            pair_[0].wait_send()
        del started[-9:]
        both = both + start(z_list[9:], *sems, lambda t: s.at[t], r.at[me_s], lambda t: r.at[t])
        r[me_s] = s[me_s]
        return both

    def start_c(phase, src_at, dst_at, own):
        both = start(c_list, col_send.at[phase], col_recv.at[phase], src_at, dst_at(me_p), dst_at)
        own()
        return both

    def pass_on(k, src, dst):
        go = pltpu.make_async_remote_copy(
            src_ref=src, dst_ref=dst, send_sem=twin_send.at[k], recv_sem=twin_recv.at[k],
            device_id=twin, device_id_type=MESH,
        )
        go.start()
        started.append((go, go))
        return started[-1:]

    def start_d(phase, s, r):
        both = start(d_list, depth_send.at[phase], depth_recv.at[phase], lambda t: s, r.at[me_d], lambda t: r.at[t])
        r[me_d] = s[...]
        return both

    slot = lax.broadcasted_iota(jnp.int32, (1, 1, LANE), 2) // SLOT
    chunk = lax.broadcasted_iota(jnp.int32, (1, 1, LANE), 2) % SLOT // PAD_LANES
    chunk2 = lax.broadcasted_iota(jnp.int32, (1, LANE), 1) % SLOT // PAD_LANES

    def padded_t(ref):
        pad[:, :k_block, :] = ref[...].astype(F32)
        pad[:, k_block:, :] = jnp.zeros((i_q, SLOT - k_block, ch), F32)
        return pad[...].reshape(width, ch).T

    def pack(x):
        return jnp.stack([lanes(x, v).reshape(n_z, hz, LANE) for v in range(vl)], axis=1).astype(BF16)

    fetch[0].wait()
    x_hat, inv_std = norm_rows(padded_t(pair))
    normed = x_hat.astype(BF16)
    fetch[1].wait()
    w_in_t = w_in[...].astype(F32).T.astype(BF16)
    fetch[2].wait()
    lane_id = lax.broadcasted_iota(jnp.int32, (1, width), 1)
    row_mask = jnp.zeros((1, width), F32)
    for i in range(i_q):
        here = mask[me_r * i_block + me_d * i_q + i].astype(F32)
        row_mask = jnp.where(lane_id // SLOT == i, here, row_mask)
    col_mask = jnp.zeros((1, width), F32)
    for t in range(k_block):
        here = mask[me_c * k_block + t].astype(F32)
        col_mask = jnp.where(lane_id % SLOT == t, here, col_mask)
    pair_mask = row_mask * col_mask
    parts = []
    for block in range(2):
        both = dot(w_in_t[2 * block * hid : 2 * (block + 1) * hid], normed)
        sig, val = jax.nn.sigmoid(both[:hid]), both[hid:]
        proj[2 * block] = sig
        proj[2 * block + 1] = val
        out = pair_mask * sig * val
        parts.append([lanes(out, v).reshape(n_z, hz, LANE) for v in range(vl)])
    s1[...] = jnp.stack(fold(*parts, chunk), axis=1).astype(BF16)

    pl.semaphore_wait(barrier, len(peers))
    move = start_z(0, s1, r1)
    for f in fetch[3:]:
        f.wait()
    cot_t = padded_t(cot)
    gate_val = jax.nn.sigmoid(dot(w_gate[...].astype(F32).T.astype(BF16), normed))
    w_out_t = w_out[...].astype(F32).T.astype(BF16)
    arrive(move)

    x = r1[...].astype(F32)
    a_tiles, b_tiles = unfold([x[:, j] for j in range(2 * vl - 1)], chunk)
    for v in range(vl):
        f1[v] = jnp.concatenate([a_tiles[v], b_tiles[v]], axis=1).reshape(n_z * 2 * hz, LANE)
    for h in range(hz):
        for v in range(vl):
            a0, b0, a1, b1 = (
                f1[v, pl.ds(dd * half * 2 * hz + block * hz + h, half, stride=2 * hz), :]
                for dd in range(2) for block in range(2)
            )
            at = slice(v * LANE, (v + 1) * LANE)
            s2[2 * h, :, at] = jnp.concatenate([b0, b1, a0, a1], axis=0).astype(BF16)
            s2[2 * h + 1, :, at] = jnp.concatenate([b0, b1, a1, a0], axis=0).astype(BF16)

    def own_2():
        r2[me_p] = s2[me_p]

    b_part, a_part = slice(0, 2 * half), slice(2 * half, 4 * half)
    move = start_c(0, lambda t: s2.at[t], lambda t: r2.at[t], own_2)
    arrive(move)
    pass_b = pass_on(0, r2.at[:, b_part], t2.at[:, b_part])
    pass_a = pass_on(1, r2.at[:, a_part], t2.at[:, a_part])
    x = r2[:, a_part, :].astype(F32)
    a_rows = to_matrix([lanes(x, v) for v in range(vl)], slot)
    a_own = jnp.concatenate([m[:half] for m in a_rows], axis=0).astype(BF16)

    def place_b(core, ref):
        x = ref[:, b_part, :].astype(F32)
        for i, m in enumerate(to_matrix([lanes(x, v) for v in range(vl)], slot)):
            for dd in range(n_dd):
                at = (dd * i_q + i) * half
                for g in range(groups):
                    bn[g, core, at : at + half, :] = lanes(m[dd * half : (dd + 1) * half], g)

    place_b(me_core, r2)
    arrive(pass_b)
    place_b(1 - me_core, t2)
    rows = []
    for core in range(2):
        for q in range(half):
            rows.append(jnp.concatenate(
                [bn[g, core, pl.ds(q, k_block, stride=half), :] for g in range(groups)], axis=-1
            ))
            rows.append(jnp.zeros((SLOT - k_block, full), F32))
    b_mat = jnp.concatenate(rows, axis=0).astype(BF16)
    tri = lax.dot_general(a_own, b_mat, (((1,), (1,)), ((), ())), preferred_element_type=F32)
    for c, x in enumerate(from_matrix(tri.reshape(i_q, half, full), slot)):
        s3[c] = x.reshape(vl * half, LANE)
    size3 = vl * half

    def rows3(t):
        return pl.ds(pl.multiple_of(t * size3, size3), size3)

    def own_3():
        r3[rows3(me_p), :] = s3[me_p]

    move = start_c(2, lambda t: s3.at[t], lambda t: r3.at[rows3(t)], own_3)

    all_a[me_core] = jnp.concatenate(a_rows, axis=0).astype(BF16)
    arrive(pass_a)
    x = t2[:, a_part, :].astype(F32)
    all_a[1 - me_core] = jnp.concatenate(to_matrix([lanes(x, v) for v in range(vl)], slot), axis=0).astype(BF16)
    arrive(move)

    for dd in range(n_dd):
        for q in range(half):
            parts = [r3[pl.ds(dd * size3 + v * half + q, hz, stride=2 * size3), :] for v in range(vl)]
            s4[dd * half + q] = jnp.stack(parts, axis=0).astype(BF16)
    move = start_z(1, s4, r4)
    arrive(move)

    x = r4[...].astype(F32)
    tri_t = jnp.concatenate([x[:, v].reshape(hid, LANE) for v in range(vl)], axis=-1)
    y_hat, tri_std = norm_rows(tri_t)
    out_proj = dot(w_out_t, y_hat.astype(BF16))
    d_o = (cot_t * gate_val).astype(BF16)
    d_y = dot(w_out[...], d_o)
    s5[...] = pack(norm_back(y_hat, tri_std, d_y))
    move = start_z(2, s5, r5)

    def natural(x):
        return x.T.reshape(i_q, SLOT, ch)[:, :k_block, :].reshape(i_q * k_block, ch).astype(BF16)

    su[...] = natural(gate_val * out_proj)
    d_gate_pre = (cot_t * out_proj * gate_val * (1.0 - gate_val)).astype(BF16)
    d_gate = dot(w_gate[...], d_gate_pre)
    arrive(move)
    update_move = start_d(0, su, ru)

    pitch = vl * hz
    f5[...] = r5[...].astype(F32).reshape(n_z * pitch, LANE)
    for h in range(hz):
        for v in range(vl):
            t0, t1 = (f5[pl.ds(dd * half * pitch + v * hz + h, half, stride=pitch), :] for dd in range(2))
            at = slice(v * LANE, (v + 1) * LANE)
            s6[2 * h, :, at] = jnp.concatenate([t0, t1], axis=0).astype(BF16)
            s6[2 * h + 1, :, at] = jnp.concatenate([t1, t0], axis=0).astype(BF16)

    def own_6():
        r6[me_p] = s6[me_p]

    move = start_c(3, lambda t: s6.at[t], lambda t: r6.at[t], own_6)
    arrive(move)
    pass_t = pass_on(2, r6, t6)
    x = r6[...].astype(F32)
    rows = to_matrix([lanes(x, v) for v in range(vl)], slot)
    for i, m in enumerate(rows):
        tgf[me_core, i] = m
    tg_own = jnp.concatenate([m[:half] for m in rows], axis=0).astype(BF16)
    grad_a = dot(tg_own, b_mat).reshape(i_q, half, full)
    arrive(pass_t)
    x = t6[...].astype(F32)
    for i, m in enumerate(to_matrix([lanes(x, v) for v in range(vl)], slot)):
        tgf[1 - me_core, i] = m
    mine = pl.ds(pl.multiple_of(me_core * (full // 2), full // 2), full // 2)
    tg_t = tgf[:, :, :, mine].reshape(2 * i_q * 2 * half, full // 2).T.astype(BF16)
    part_b = dot(tg_t, all_a[...].reshape(2 * i_q * 2 * half, full))
    for g in range(groups):
        gf[g] = lanes(part_b, g)
    rows = []
    for i in range(i_q):
        rows.append(grad_a[i])
        rows.append(jnp.concatenate(
            [gf[g, pl.ds(me_dd * i_q + i, half, stride=SLOT), :] for g in range(groups)], axis=-1
        ))
    both = jnp.concatenate(rows, axis=0).reshape(i_q, 2 * half, full)
    for c, x in enumerate(from_matrix(both, slot)):
        for v in range(vl):
            s8[c, :, v * LANE : (v + 1) * LANE] = x[v].astype(BF16)

    def own_8():
        r8[me_p] = s8[me_p]

    move = start_c(4, lambda t: s8.at[t], lambda t: r8.at[t], own_8)
    arrive(move)
    x = r8[...].astype(F32)
    for v in range(vl):
        f8[v] = lanes(x, v).reshape(n_c * 2 * half, LANE)
    for dd in range(n_dd):
        for q in range(half):
            a_tiles, b_tiles = (
                [f8[v, pl.ds((dd * 2 + block) * half + q, hz, stride=4 * half), :] for v in range(vl)]
                for block in range(2)
            )
            s9[dd * half + q] = jnp.stack(fold(a_tiles, b_tiles, chunk2), axis=0).astype(BF16)
    move = start_z(3, s9, r9)
    arrive(move)

    d_normed = d_gate
    x = r9[...].astype(F32)
    grads = unfold([x[:, j] for j in range(2 * vl - 1)], chunk)
    for block in range(2):
        grad = jnp.concatenate([g.reshape(hid, LANE) for g in grads[block]], axis=-1) * pair_mask
        sig, val = proj[2 * block], proj[2 * block + 1]
        d_pre = (grad * val * sig * (1.0 - sig)).astype(BF16)
        d_val = (grad * sig).astype(BF16)
        d_normed = d_normed + dot(w_in[:, 2 * block * hid : (2 * block + 1) * hid], d_pre)
        d_normed = d_normed + dot(w_in[:, (2 * block + 1) * hid : (2 * block + 2) * hid], d_val)
    sg[...] = natural(norm_back(x_hat, inv_std, d_normed))
    move = start_d(1, sg, rg)
    arrive(update_move)
    for d in range(n_d):
        update_out[d * i_q : (d + 1) * i_q] = ru[d].astype(F32).reshape(i_q, k_block, ch).astype(BF16)
    arrive(move)
    for d in range(n_d):
        grad_out[d * i_q : (d + 1) * i_q] = rg[d].astype(F32).reshape(i_q, k_block, ch).astype(BF16)
    for go, _ in started:
        go.wait_send()


def shards(sizes, pair, cotangent, w_in, w_gate, w_out, residue_mask):
    n_d, n_r, n_c = sizes
    n_x = 4 if n_c == 16 else 2
    i_block, k_block, ch = pair.shape
    hid = w_out.shape[0]
    i_q = i_block // n_d
    width = i_q * SLOT
    vl = width // LANE
    n_z = (n_r // 2) * n_d
    half = n_r
    hz = hid // n_z
    full = n_c * SLOT
    groups = max(full // LANE, 1)
    pitch = vl * hz
    vm = pltpu.VMEM
    scratch = [
        pltpu.SMEM(residue_mask.shape, jnp.int32),
        vm((i_q, k_block, ch), BF16),
        vm((i_q, k_block, ch), BF16),
        vm(w_in.shape, BF16),
        vm(w_gate.shape, BF16),
        vm(w_out.shape, BF16),
        pltpu.SemaphoreType.DMA((6,)),
        vm((i_q, SLOT, ch), F32),
        vm((4, hid, width), F32),
        vm((n_z, 2 * vl - 1, hz, LANE), BF16),
        vm((n_z, 2 * vl - 1, hz, LANE), BF16),
        vm((vl, n_z * 2 * hz, LANE), F32),
        vm((n_c, 4 * half, width), BF16),
        vm((n_c, 4 * half, width), BF16),
        vm((n_c, 4 * half, width), BF16),
        vm((groups, 2, k_block * half, LANE), F32),
        vm((2, i_q * 2 * half, full), BF16),
        vm((n_c, vl * half, LANE), F32),
        vm((n_c * vl * half, LANE), F32),
        vm((n_z, vl, hz, LANE), BF16),
        vm((n_z, vl, hz, LANE), BF16),
        vm((n_z, vl, hz, LANE), BF16),
        vm((n_z, vl, hz, LANE), BF16),
        vm((n_z * pitch, LANE), F32),
        vm((n_c, 2 * half, width), BF16),
        vm((n_c, 2 * half, width), BF16),
        vm((n_c, 2 * half, width), BF16),
        vm((2, i_q, 2 * half, full), F32),
        vm((groups, full // 2, LANE), F32),
        vm((n_c, 2 * half, width), BF16),
        vm((n_c, 2 * half, width), BF16),
        vm((vl, n_c * 2 * half, LANE), F32),
        vm((n_z, 2 * vl - 1, hz, LANE), BF16),
        vm((n_z, 2 * vl - 1, hz, LANE), BF16),
        vm((i_q * k_block, ch), BF16),
        vm((n_d, i_q * k_block, ch), BF16),
        vm((i_q * k_block, ch), BF16),
        vm((n_d, i_q * k_block, ch), BF16),
    ]
    for phases, size in ((4, n_z), (5, n_c), (2, n_d)):
        scratch += [pltpu.SemaphoreType.DMA((phases, size))] * 2
    scratch += [pltpu.SemaphoreType.DMA((3,))] * 2
    whole = pl.BlockSpec(memory_space=pltpu.VMEM)
    return pl.pallas_call(
        functools.partial(kernel, (n_d, n_r, n_c, n_x, i_block, k_block, ch, hid)),
        out_shape=(jax.ShapeDtypeStruct(pair.shape, BF16),) * 2,
        in_specs=[pl.BlockSpec(memory_space=pl.ANY)] * 6,
        out_specs=(whole, whole),
        scratch_shapes=scratch,
        compiler_params=pltpu.CompilerParams(
            collective_id=0, has_side_effects=True, vmem_limit_bytes=60 * 1024 * 1024
        ),
    )(residue_mask, pair, cotangent, w_in, w_gate, w_out)


def solution(mesh):
    in_specs = (P("row", "col", None), P("row", "col", None), P(), P(), P(), P())
    out_specs = (P("row", "col", None), P("row", "col", None))
    sizes = (mesh.shape["depth"], mesh.shape["row"], mesh.shape["col"])
    return jax.shard_map(
        functools.partial(shards, sizes), mesh=mesh, in_specs=in_specs, out_specs=out_specs, check_vma=False
    )
```

```python
import functools

import jax
import jax.numpy as jnp
from jax import lax
from jax.experimental import pallas as pl
from jax.experimental.pallas import tpu as pltpu
from jax.sharding import PartitionSpec as P

MESH = pl.DeviceIdType.MESH
F32 = jnp.float32
BF16 = jnp.bfloat16
SLOT = 32
LANE = 128
PER = LANE // SLOT
PAD_LANES = 8


def dot(left, right):
    return jnp.dot(left, right, preferred_element_type=F32)


def norm_rows(values):
    average = jnp.mean(values, axis=0, keepdims=True)
    centered = values - average
    variance = jnp.mean(centered * centered, axis=0, keepdims=True)
    inv_std = lax.rsqrt(variance + 1e-05)
    return (centered * inv_std, inv_std)


def norm_back(x_hat, inv_std, upstream):
    first = jnp.mean(upstream, axis=0, keepdims=True)
    second = jnp.mean(upstream * x_hat, axis=0, keepdims=True)
    return inv_std * (upstream - first - x_hat * second)


def lanes(x, v):
    return x[..., v * LANE : (v + 1) * LANE]


def to_matrix(tiles, slot):
    out = []
    for x in tiles:
        groups, rows = x.shape[0] // PER, x.shape[1]
        x = x.reshape(groups, PER, rows, LANE)
        for s in range(PER):
            acc = None
            for c in range(PER):
                y = x[:, c]
                if c != s:
                    y = pltpu.roll(y, (SLOT * (c - s)) % LANE, 2)
                acc = y if acc is None else jnp.where(slot == c, y, acc)
            out.append(jnp.concatenate([acc[g] for g in range(groups)], axis=-1))
    return out


def fold(a, b, chunk):
    last, per_slot = b[-1], SLOT // PAD_LANES
    out = []
    for j, tile in enumerate(a):
        moved = pltpu.roll(last, PAD_LANES * (per_slot - 1 - j), last.ndim - 1)
        out.append(jnp.where(chunk == per_slot - 1, moved, tile))
    return out + b[:-1]


def unfold(tiles, chunk):
    per_slot = SLOT // PAD_LANES
    last = jnp.zeros_like(tiles[0])
    a = []
    for j, tile in enumerate(tiles[: per_slot - 1]):
        moved = pltpu.roll(tile, LANE - PAD_LANES * (per_slot - 1 - j), tile.ndim - 1)
        last = jnp.where(chunk == j, moved, last)
        a.append(jnp.where(chunk == per_slot - 1, 0.0, tile))
    return a, tiles[per_slot - 1 :] + [last]


def from_matrix(matrix, slot):
    count, rows, width = matrix.shape
    x = matrix.reshape(count // PER, PER, rows, width)
    out = []
    for g in range(width // LANE):
        part = lanes(x, g)
        for c in range(PER):
            acc = None
            for s in range(PER):
                y = part[:, s]
                if c != s:
                    y = pltpu.roll(y, (SLOT * (s - c)) % LANE, 2)
                acc = y if acc is None else jnp.where(slot == s, y, acc)
            out.append(acc)
    return out


def kernel(
    dims,
    mask_hbm, pair_hbm, cot_hbm, w_in_hbm, w_gate_hbm, w_out_hbm,
    update_out, grad_out,
    mask, pair, cot, w_in, w_gate, w_out, in_sem,
    pad, proj, s1, r1, f1, s2, r2, t2, bn, all_a, s3, r3, s4, r4, s5, r5, f5, s6, r6, t6, tgf,
    gf, s8, r8, f8, s9, r9, su, ru, sg, rg,
    z_send, z_recv, col_send, col_recv, depth_send, depth_recv, over_send, over_recv, twin_send, twin_recv,
):
    n_d, n_r, n_c, n_x, i_block, k_block, ch, hid = dims
    n_zh, n_dd, n_y = n_r // 2, n_d // 2, n_c // n_x
    n_z = n_zh * n_d
    hz = hid // n_z
    i_q = i_block // n_d
    width = i_q * SLOT
    vl = width // LANE
    half = 2 * n_zh
    full = n_c * SLOT
    groups = full // LANE
    me_d, me_r, me_c = lax.axis_index("depth"), lax.axis_index("row"), lax.axis_index("col")
    me_zh, me_core = me_r // 2, me_r % 2

    def z_slot(zh, d):
        return (d % n_dd) * half + (d // n_dd) * n_zh + zh

    def c_slot(c):
        return ((c // 2) % 2) * half + (c % 2) * n_zh + c // 4

    me_s, me_p = z_slot(me_zh, me_d), c_slot(me_c)
    me_dd = me_p % 2

    def z_peer(o):
        z = lax.rem(me_zh * n_d + me_d + o + n_z, n_z)
        zh, d = z // n_d, z % n_d
        return {"row": zh * 2 + me_core, "depth": d}, z_slot(zh, d)

    def c_peer(ox, oy):
        x = lax.rem(me_c // n_y + ox + n_x, n_x)
        y = lax.rem(me_c % n_y + oy + n_y, n_y)
        c = x * n_y + y
        return {"col": c}, c_slot(c)

    def d_peer(o):
        d = lax.rem(me_d + o + n_d, n_d)
        return {"depth": d}, d

    z_offsets = sorted(range(1, n_z), key=lambda o: -min(o, n_z - o))
    c_offsets = sorted(
        [(x, y) for x in range(n_x) for y in range(n_y)],
        key=lambda o: -(min(o[0], n_x - o[0]) + min(o[1], n_y - o[1])),
    )
    d_offsets = list(range(1, n_d))

    z_list = [z_peer(o) + (z_peer(-o)[1], k) for k, o in enumerate(z_offsets)]
    d_list = [d_peer(o) + (d_peer(-o)[1], k) for k, o in enumerate(d_offsets)]
    c_list = [
        c_peer(ox, oy) + (c_peer(-ox, -oy)[1], k) for k, (ox, oy) in enumerate(c_offsets) if (ox, oy) != (0, 0)
    ]
    x_list = []
    for k, (ox, oy) in enumerate(c_offsets):
        to, slot_to = c_peer(ox, oy)
        x_list.append(({**to, "row": me_zh * 2 + 1 - me_core}, slot_to, c_peer(-ox, -oy)[1], k))
    twin = {"row": me_zh * 2 + 1 - me_core}

    barrier = pltpu.get_barrier_semaphore()
    peers = [to for to, _, _, _ in z_list + c_list + x_list]
    for to in peers:
        pl.semaphore_signal(barrier, inc=1, device_id=to, device_id_type=MESH)

    own_rows = pl.ds(me_d * i_q, i_q)
    fetch = [
        pltpu.make_async_copy(a, b, in_sem.at[k])
        for k, (a, b) in enumerate([
            (pair_hbm.at[own_rows], pair), (w_in_hbm, w_in), (mask_hbm, mask),
            (cot_hbm.at[own_rows], cot), (w_gate_hbm, w_gate), (w_out_hbm, w_out),
        ])
    ]
    for f in fetch:
        f.start()

    started = []

    def start(peer_list, send, recv, src_at, dst_mine, dst_from):
        both = []
        for to, slot_to, slot_from, k in peer_list:
            go = pltpu.make_async_remote_copy(
                src_ref=src_at(slot_to), dst_ref=dst_mine, send_sem=send.at[k], recv_sem=recv.at[k],
                device_id=to, device_id_type=MESH,
            )
            come = pltpu.make_async_remote_copy(
                src_ref=src_at(slot_to), dst_ref=dst_from(slot_from), send_sem=send.at[k], recv_sem=recv.at[k],
                device_id=to, device_id_type=MESH,
            )
            go.start()
            both.append((go, come))
        started.extend(both)
        return both

    def arrive(both):
        for _, come in both:
            come.wait_recv()

    def start_z(phase, s, r):
        sems = (z_send.at[phase], z_recv.at[phase])
        both = start(z_list[:9], *sems, lambda t: s.at[t], r.at[me_s], lambda t: r.at[t])
        for pair_ in both:
            pair_[0].wait_send()
        del started[-9:]
        both = both + start(z_list[9:], *sems, lambda t: s.at[t], r.at[me_s], lambda t: r.at[t])
        r[me_s] = s[me_s]
        return both

    def start_c(phase, src_at, dst_at, own):
        both = start(c_list, col_send.at[phase], col_recv.at[phase], src_at, dst_at(me_p), dst_at)
        own()
        return both

    def pass_on(k, src, dst):
        go = pltpu.make_async_remote_copy(
            src_ref=src, dst_ref=dst, send_sem=twin_send.at[k], recv_sem=twin_recv.at[k],
            device_id=twin, device_id_type=MESH,
        )
        go.start()
        started.append((go, go))
        return started[-1:]

    def start_d(phase, s, r):
        both = start(d_list, depth_send.at[phase], depth_recv.at[phase], lambda t: s, r.at[me_d], lambda t: r.at[t])
        r[me_d] = s[...]
        return both

    slot = lax.broadcasted_iota(jnp.int32, (1, 1, LANE), 2) // SLOT
    chunk = lax.broadcasted_iota(jnp.int32, (1, 1, LANE), 2) % SLOT // PAD_LANES
    chunk2 = lax.broadcasted_iota(jnp.int32, (1, LANE), 1) % SLOT // PAD_LANES

    def padded_t(ref):
        pad[:, :k_block, :] = ref[...].astype(F32)
        pad[:, k_block:, :] = jnp.zeros((i_q, SLOT - k_block, ch), F32)
        return pad[...].reshape(width, ch).T

    def pack(x):
        return jnp.stack([lanes(x, v).reshape(n_z, hz, LANE) for v in range(vl)], axis=1).astype(BF16)

    fetch[0].wait()
    x_hat, inv_std = norm_rows(padded_t(pair))
    normed = x_hat.astype(BF16)
    fetch[1].wait()
    w_in_t = w_in[...].astype(F32).T.astype(BF16)
    fetch[2].wait()
    lane_id = lax.broadcasted_iota(jnp.int32, (1, width), 1)
    row_mask = jnp.zeros((1, width), F32)
    for i in range(i_q):
        here = mask[me_r * i_block + me_d * i_q + i].astype(F32)
        row_mask = jnp.where(lane_id // SLOT == i, here, row_mask)
    col_mask = jnp.zeros((1, width), F32)
    for t in range(k_block):
        here = mask[me_c * k_block + t].astype(F32)
        col_mask = jnp.where(lane_id % SLOT == t, here, col_mask)
    pair_mask = row_mask * col_mask
    parts = []
    for block in range(2):
        both = dot(w_in_t[2 * block * hid : 2 * (block + 1) * hid], normed)
        sig, val = jax.nn.sigmoid(both[:hid]), both[hid:]
        proj[2 * block] = sig
        proj[2 * block + 1] = val
        out = pair_mask * sig * val
        parts.append([lanes(out, v).reshape(n_z, hz, LANE) for v in range(vl)])
    s1[...] = jnp.stack(fold(*parts, chunk), axis=1).astype(BF16)

    pl.semaphore_wait(barrier, len(peers))
    move = start_z(0, s1, r1)
    for f in fetch[3:]:
        f.wait()
    cot_t = padded_t(cot)
    gate_val = jax.nn.sigmoid(dot(w_gate[...].astype(F32).T.astype(BF16), normed))
    w_out_t = w_out[...].astype(F32).T.astype(BF16)
    arrive(move)

    x = r1[...].astype(F32)
    a_tiles, b_tiles = unfold([x[:, j] for j in range(2 * vl - 1)], chunk)
    for v in range(vl):
        f1[v] = jnp.concatenate([a_tiles[v], b_tiles[v]], axis=1).reshape(n_z * 2 * hz, LANE)
    for h in range(hz):
        for v in range(vl):
            a0, b0, a1, b1 = (
                f1[v, pl.ds(dd * half * 2 * hz + block * hz + h, half, stride=2 * hz), :]
                for dd in range(2) for block in range(2)
            )
            at = slice(v * LANE, (v + 1) * LANE)
            s2[2 * h, :, at] = jnp.concatenate([b0, b1, a0, a1], axis=0).astype(BF16)
            s2[2 * h + 1, :, at] = jnp.concatenate([b0, b1, a1, a0], axis=0).astype(BF16)

    def own_2():
        r2[me_p] = s2[me_p]

    b_part, a_part = slice(0, 2 * half), slice(2 * half, 4 * half)
    pass_b = start(
        x_list, over_send.at[0], over_recv.at[0],
        lambda t: s2.at[t, b_part], t2.at[me_p, b_part], lambda t: t2.at[t, b_part],
    )
    move = start_c(0, lambda t: s2.at[t], lambda t: r2.at[t], own_2)
    arrive(move)
    pass_a = pass_on(1, r2.at[:, a_part], t2.at[:, a_part])
    x = r2[:, a_part, :].astype(F32)
    a_rows = to_matrix([lanes(x, v) for v in range(vl)], slot)
    a_own = jnp.concatenate([m[:half] for m in a_rows], axis=0).astype(BF16)

    def place_b(core, ref):
        x = ref[:, b_part, :].astype(F32)
        for i, m in enumerate(to_matrix([lanes(x, v) for v in range(vl)], slot)):
            for dd in range(n_dd):
                at = (dd * i_q + i) * half
                for g in range(groups):
                    bn[g, core, at : at + half, :] = lanes(m[dd * half : (dd + 1) * half], g)

    place_b(me_core, r2)
    arrive(pass_b)
    place_b(1 - me_core, t2)
    rows = []
    for core in range(2):
        for q in range(half):
            rows.append(jnp.concatenate(
                [bn[g, core, pl.ds(q, k_block, stride=half), :] for g in range(groups)], axis=-1
            ))
            rows.append(jnp.zeros((SLOT - k_block, full), F32))
    b_mat = jnp.concatenate(rows, axis=0).astype(BF16)
    tri = lax.dot_general(a_own, b_mat, (((1,), (1,)), ((), ())), preferred_element_type=F32)
    for c, x in enumerate(from_matrix(tri.reshape(i_q, half, full), slot)):
        s3[c] = x.reshape(vl * half, LANE)
    size3 = vl * half

    def rows3(t):
        return pl.ds(pl.multiple_of(t * size3, size3), size3)

    def own_3():
        r3[rows3(me_p), :] = s3[me_p]

    move = start_c(2, lambda t: s3.at[t], lambda t: r3.at[rows3(t)], own_3)

    all_a[me_core] = jnp.concatenate(a_rows, axis=0).astype(BF16)
    arrive(pass_a)
    x = t2[:, a_part, :].astype(F32)
    all_a[1 - me_core] = jnp.concatenate(to_matrix([lanes(x, v) for v in range(vl)], slot), axis=0).astype(BF16)
    arrive(move)

    for dd in range(n_dd):
        for q in range(half):
            parts = [r3[pl.ds(dd * size3 + v * half + q, hz, stride=2 * size3), :] for v in range(vl)]
            s4[dd * half + q] = jnp.stack(parts, axis=0).astype(BF16)
    move = start_z(1, s4, r4)
    arrive(move)

    x = r4[...].astype(F32)
    tri_t = jnp.concatenate([x[:, v].reshape(hid, LANE) for v in range(vl)], axis=-1)
    y_hat, tri_std = norm_rows(tri_t)
    out_proj = dot(w_out_t, y_hat.astype(BF16))
    d_o = (cot_t * gate_val).astype(BF16)
    d_y = dot(w_out[...], d_o)
    s5[...] = pack(norm_back(y_hat, tri_std, d_y))
    move = start_z(2, s5, r5)

    def natural(x):
        return x.T.reshape(i_q, SLOT, ch)[:, :k_block, :].reshape(i_q * k_block, ch).astype(BF16)

    su[...] = natural(gate_val * out_proj)
    d_gate_pre = (cot_t * out_proj * gate_val * (1.0 - gate_val)).astype(BF16)
    d_gate = dot(w_gate[...], d_gate_pre)
    arrive(move)
    update_move = start_d(0, su, ru)

    pitch = vl * hz
    f5[...] = r5[...].astype(F32).reshape(n_z * pitch, LANE)
    for h in range(hz):
        for v in range(vl):
            t0, t1 = (f5[pl.ds(dd * half * pitch + v * hz + h, half, stride=pitch), :] for dd in range(2))
            at = slice(v * LANE, (v + 1) * LANE)
            s6[2 * h, :, at] = jnp.concatenate([t0, t1], axis=0).astype(BF16)
            s6[2 * h + 1, :, at] = jnp.concatenate([t1, t0], axis=0).astype(BF16)

    def own_6():
        r6[me_p] = s6[me_p]

    pass_t = start(x_list, over_send.at[1], over_recv.at[1], lambda t: s6.at[t], t6.at[me_p], lambda t: t6.at[t])
    move = start_c(3, lambda t: s6.at[t], lambda t: r6.at[t], own_6)
    arrive(move)
    x = r6[...].astype(F32)
    rows = to_matrix([lanes(x, v) for v in range(vl)], slot)
    for i, m in enumerate(rows):
        tgf[me_core, i] = m
    tg_own = jnp.concatenate([m[:half] for m in rows], axis=0).astype(BF16)
    grad_a = dot(tg_own, b_mat).reshape(i_q, half, full)
    arrive(pass_t)
    x = t6[...].astype(F32)
    for i, m in enumerate(to_matrix([lanes(x, v) for v in range(vl)], slot)):
        tgf[1 - me_core, i] = m
    mine = pl.ds(pl.multiple_of(me_core * (full // 2), full // 2), full // 2)
    tg_t = tgf[:, :, :, mine].reshape(2 * i_q * 2 * half, full // 2).T.astype(BF16)
    part_b = dot(tg_t, all_a[...].reshape(2 * i_q * 2 * half, full))
    for g in range(groups):
        gf[g] = lanes(part_b, g)
    rows = []
    for i in range(i_q):
        rows.append(grad_a[i])
        rows.append(jnp.concatenate(
            [gf[g, pl.ds(me_dd * i_q + i, half, stride=SLOT), :] for g in range(groups)], axis=-1
        ))
    both = jnp.concatenate(rows, axis=0).reshape(i_q, 2 * half, full)
    for c, x in enumerate(from_matrix(both, slot)):
        for v in range(vl):
            s8[c, :, v * LANE : (v + 1) * LANE] = x[v].astype(BF16)

    def own_8():
        r8[me_p] = s8[me_p]

    move = start_c(4, lambda t: s8.at[t], lambda t: r8.at[t], own_8)
    arrive(move)
    x = r8[...].astype(F32)
    for v in range(vl):
        f8[v] = lanes(x, v).reshape(n_c * 2 * half, LANE)
    for dd in range(n_dd):
        for q in range(half):
            a_tiles, b_tiles = (
                [f8[v, pl.ds((dd * 2 + block) * half + q, hz, stride=4 * half), :] for v in range(vl)]
                for block in range(2)
            )
            s9[dd * half + q] = jnp.stack(fold(a_tiles, b_tiles, chunk2), axis=0).astype(BF16)
    move = start_z(3, s9, r9)
    arrive(move)

    d_normed = d_gate
    x = r9[...].astype(F32)
    grads = unfold([x[:, j] for j in range(2 * vl - 1)], chunk)
    for block in range(2):
        grad = jnp.concatenate([g.reshape(hid, LANE) for g in grads[block]], axis=-1) * pair_mask
        sig, val = proj[2 * block], proj[2 * block + 1]
        d_pre = (grad * val * sig * (1.0 - sig)).astype(BF16)
        d_val = (grad * sig).astype(BF16)
        d_normed = d_normed + dot(w_in[:, 2 * block * hid : (2 * block + 1) * hid], d_pre)
        d_normed = d_normed + dot(w_in[:, (2 * block + 1) * hid : (2 * block + 2) * hid], d_val)
    sg[...] = natural(norm_back(x_hat, inv_std, d_normed))
    move = start_d(1, sg, rg)
    arrive(update_move)
    for d in range(n_d):
        update_out[d * i_q : (d + 1) * i_q] = ru[d].astype(F32).reshape(i_q, k_block, ch).astype(BF16)
    arrive(move)
    for d in range(n_d):
        grad_out[d * i_q : (d + 1) * i_q] = rg[d].astype(F32).reshape(i_q, k_block, ch).astype(BF16)
    for go, _ in started:
        go.wait_send()


def shards(sizes, pair, cotangent, w_in, w_gate, w_out, residue_mask):
    n_d, n_r, n_c = sizes
    n_x = 4 if n_c == 16 else 2
    i_block, k_block, ch = pair.shape
    hid = w_out.shape[0]
    i_q = i_block // n_d
    width = i_q * SLOT
    vl = width // LANE
    n_z = (n_r // 2) * n_d
    half = n_r
    hz = hid // n_z
    full = n_c * SLOT
    groups = max(full // LANE, 1)
    pitch = vl * hz
    vm = pltpu.VMEM
    operands = [
        pltpu.with_memory_space_constraint(v, pltpu.HBM)
        for v in (residue_mask, pair, cotangent, w_in, w_gate, w_out)
    ]
    scratch = [
        pltpu.SMEM(residue_mask.shape, jnp.int32),
        vm((i_q, k_block, ch), BF16),
        vm((i_q, k_block, ch), BF16),
        vm(w_in.shape, BF16),
        vm(w_gate.shape, BF16),
        vm(w_out.shape, BF16),
        pltpu.SemaphoreType.DMA((6,)),
        vm((i_q, SLOT, ch), F32),
        vm((4, hid, width), F32),
        vm((n_z, 2 * vl - 1, hz, LANE), BF16),
        vm((n_z, 2 * vl - 1, hz, LANE), BF16),
        vm((vl, n_z * 2 * hz, LANE), F32),
        vm((n_c, 4 * half, width), BF16),
        vm((n_c, 4 * half, width), BF16),
        vm((n_c, 4 * half, width), BF16),
        vm((groups, 2, k_block * half, LANE), F32),
        vm((2, i_q * 2 * half, full), BF16),
        vm((n_c, vl * half, LANE), F32),
        vm((n_c * vl * half, LANE), F32),
        vm((n_z, vl, hz, LANE), BF16),
        vm((n_z, vl, hz, LANE), BF16),
        vm((n_z, vl, hz, LANE), BF16),
        vm((n_z, vl, hz, LANE), BF16),
        vm((n_z * pitch, LANE), F32),
        vm((n_c, 2 * half, width), BF16),
        vm((n_c, 2 * half, width), BF16),
        vm((n_c, 2 * half, width), BF16),
        vm((2, i_q, 2 * half, full), F32),
        vm((groups, full // 2, LANE), F32),
        vm((n_c, 2 * half, width), BF16),
        vm((n_c, 2 * half, width), BF16),
        vm((vl, n_c * 2 * half, LANE), F32),
        vm((n_z, 2 * vl - 1, hz, LANE), BF16),
        vm((n_z, 2 * vl - 1, hz, LANE), BF16),
        vm((i_q * k_block, ch), BF16),
        vm((n_d, i_q * k_block, ch), BF16),
        vm((i_q * k_block, ch), BF16),
        vm((n_d, i_q * k_block, ch), BF16),
    ]
    for phases, size in ((4, n_z), (5, n_c), (2, n_d)):
        scratch += [pltpu.SemaphoreType.DMA((phases, size))] * 2
    scratch += [pltpu.SemaphoreType.DMA((2, n_c))] * 2
    scratch += [pltpu.SemaphoreType.DMA((3,))] * 2
    whole = pl.BlockSpec(memory_space=pltpu.VMEM)
    return pl.pallas_call(
        functools.partial(kernel, (n_d, n_r, n_c, n_x, i_block, k_block, ch, hid)),
        out_shape=(jax.ShapeDtypeStruct(pair.shape, BF16),) * 2,
        in_specs=[pl.BlockSpec(memory_space=pl.ANY)] * 6,
        out_specs=(whole, whole),
        scratch_shapes=scratch,
        compiler_params=pltpu.CompilerParams(
            collective_id=0, has_side_effects=True, vmem_limit_bytes=40 * 1024 * 1024
        ),
    )(*operands)


def solution(mesh):
    in_specs = (P("row", "col", None), P("row", "col", None), P(), P(), P(), P())
    out_specs = (P("row", "col", None), P("row", "col", None))
    sizes = (mesh.shape["depth"], mesh.shape["row"], mesh.shape["col"])
    return jax.shard_map(
        functools.partial(shards, sizes), mesh=mesh, in_specs=in_specs, out_specs=out_specs, check_vma=False
    )
```

```python
import functools

import jax
import jax.numpy as jnp
from jax import lax
from jax.experimental import pallas as pl
from jax.experimental.pallas import tpu as pltpu
from jax.sharding import PartitionSpec as P

MESH = pl.DeviceIdType.MESH
F32 = jnp.float32
BF16 = jnp.bfloat16
SLOT = 32
LANE = 128
PER = LANE // SLOT
PAD_LANES = 8


def dot(left, right):
    return jnp.dot(left, right, preferred_element_type=F32)


def norm_rows(values):
    average = jnp.mean(values, axis=0, keepdims=True)
    centered = values - average
    variance = jnp.mean(centered * centered, axis=0, keepdims=True)
    inv_std = lax.rsqrt(variance + 1e-05)
    return (centered * inv_std, inv_std)


def norm_back(x_hat, inv_std, upstream):
    first = jnp.mean(upstream, axis=0, keepdims=True)
    second = jnp.mean(upstream * x_hat, axis=0, keepdims=True)
    return inv_std * (upstream - first - x_hat * second)


def lanes(x, v):
    return x[..., v * LANE : (v + 1) * LANE]


def to_matrix(tiles, slot):
    out = []
    for x in tiles:
        groups, rows = x.shape[0] // PER, x.shape[1]
        x = x.reshape(groups, PER, rows, LANE)
        for s in range(PER):
            acc = None
            for c in range(PER):
                y = x[:, c]
                if c != s:
                    y = pltpu.roll(y, (SLOT * (c - s)) % LANE, 2)
                acc = y if acc is None else jnp.where(slot == c, y, acc)
            out.append(jnp.concatenate([acc[g] for g in range(groups)], axis=-1))
    return out


def fold(a, b, chunk):
    last, per_slot = b[-1], SLOT // PAD_LANES
    out = []
    for j, tile in enumerate(a):
        moved = pltpu.roll(last, PAD_LANES * (per_slot - 1 - j), last.ndim - 1)
        out.append(jnp.where(chunk == per_slot - 1, moved, tile))
    return out + b[:-1]


def unfold(tiles, chunk):
    per_slot = SLOT // PAD_LANES
    last = jnp.zeros_like(tiles[0])
    a = []
    for j, tile in enumerate(tiles[: per_slot - 1]):
        moved = pltpu.roll(tile, LANE - PAD_LANES * (per_slot - 1 - j), tile.ndim - 1)
        last = jnp.where(chunk == j, moved, last)
        a.append(jnp.where(chunk == per_slot - 1, 0.0, tile))
    return a, tiles[per_slot - 1 :] + [last]


def from_matrix(matrix, slot):
    count, rows, width = matrix.shape
    x = matrix.reshape(count // PER, PER, rows, width)
    out = []
    for g in range(width // LANE):
        part = lanes(x, g)
        for c in range(PER):
            acc = None
            for s in range(PER):
                y = part[:, s]
                if c != s:
                    y = pltpu.roll(y, (SLOT * (s - c)) % LANE, 2)
                acc = y if acc is None else jnp.where(slot == s, y, acc)
            out.append(acc)
    return out


def kernel(
    dims,
    mask_hbm, pair_hbm, cot_hbm, w_in_hbm, w_gate_hbm, w_out_hbm,
    update_out, grad_out,
    mask, pair, cot, w_in, w_gate, w_out, in_sem,
    pad, proj, s1, r1, f1, s2, r2, t2, bn, all_a, s3, r3, f3, s4, r4, s5, r5, f5, s6, r6, t6, tgf,
    gf, s8, r8, f8, s9, r9, su, ru, sg, rg,
    z_send, z_recv, col_send, col_recv, depth_send, depth_recv, over_send, over_recv, twin_send, twin_recv,
):
    n_d, n_r, n_c, n_x, i_block, k_block, ch, hid = dims
    n_zh, n_dd, n_y = n_r // 2, n_d // 2, n_c // n_x
    n_z = n_zh * n_d
    hz = hid // n_z
    i_q = i_block // n_d
    width = i_q * SLOT
    vl = width // LANE
    half = 2 * n_zh
    full = n_c * SLOT
    groups = full // LANE
    me_d, me_r, me_c = lax.axis_index("depth"), lax.axis_index("row"), lax.axis_index("col")
    me_zh, me_core = me_r // 2, me_r % 2

    def z_slot(zh, d):
        return (d % n_dd) * half + (d // n_dd) * n_zh + zh

    def c_slot(c):
        return ((c // 2) % 2) * half + (c % 2) * n_zh + c // 4

    me_s, me_p = z_slot(me_zh, me_d), c_slot(me_c)
    me_dd = me_p % 2

    def z_peer(o):
        z = lax.rem(me_zh * n_d + me_d + o + n_z, n_z)
        zh, d = z // n_d, z % n_d
        return {"row": zh * 2 + me_core, "depth": d}, z_slot(zh, d)

    def c_peer(ox, oy):
        x = lax.rem(me_c // n_y + ox + n_x, n_x)
        y = lax.rem(me_c % n_y + oy + n_y, n_y)
        c = x * n_y + y
        return {"col": c}, c_slot(c)

    def d_peer(o):
        d = lax.rem(me_d + o + n_d, n_d)
        return {"depth": d}, d

    z_offsets = sorted(range(1, n_z), key=lambda o: -min(o, n_z - o))
    c_offsets = sorted(
        [(x, y) for x in range(n_x) for y in range(n_y)],
        key=lambda o: -(min(o[0], n_x - o[0]) + min(o[1], n_y - o[1])),
    )
    d_offsets = list(range(1, n_d))

    z_list = [z_peer(o) + (z_peer(-o)[1], k) for k, o in enumerate(z_offsets)]
    d_list = [d_peer(o) + (d_peer(-o)[1], k) for k, o in enumerate(d_offsets)]
    c_list = [
        c_peer(ox, oy) + (c_peer(-ox, -oy)[1], k) for k, (ox, oy) in enumerate(c_offsets) if (ox, oy) != (0, 0)
    ]
    x_list = []
    for k, (ox, oy) in enumerate(c_offsets):
        to, slot_to = c_peer(ox, oy)
        x_list.append(({**to, "row": me_zh * 2 + 1 - me_core}, slot_to, c_peer(-ox, -oy)[1], k))
    twin = {"row": me_zh * 2 + 1 - me_core}

    barrier = pltpu.get_barrier_semaphore()
    peers = [to for to, _, _, _ in z_list + c_list + x_list]
    for to in peers:
        pl.semaphore_signal(barrier, inc=1, device_id=to, device_id_type=MESH)

    own_rows = pl.ds(me_d * i_q, i_q)
    fetch = [
        pltpu.make_async_copy(a, b, in_sem.at[k])
        for k, (a, b) in enumerate([
            (pair_hbm.at[own_rows], pair), (w_in_hbm, w_in), (mask_hbm, mask),
            (cot_hbm.at[own_rows], cot), (w_gate_hbm, w_gate), (w_out_hbm, w_out),
        ])
    ]
    for f in fetch:
        f.start()

    started = []

    def start(peer_list, send, recv, src_at, dst_mine, dst_from):
        both = []
        for to, slot_to, slot_from, k in peer_list:
            go = pltpu.make_async_remote_copy(
                src_ref=src_at(slot_to), dst_ref=dst_mine, send_sem=send.at[k], recv_sem=recv.at[k],
                device_id=to, device_id_type=MESH,
            )
            come = pltpu.make_async_remote_copy(
                src_ref=src_at(slot_to), dst_ref=dst_from(slot_from), send_sem=send.at[k], recv_sem=recv.at[k],
                device_id=to, device_id_type=MESH,
            )
            go.start()
            both.append((go, come))
        started.extend(both)
        return both

    def arrive(both):
        for _, come in both:
            come.wait_recv()

    def start_z(phase, s, r):
        sems = (z_send.at[phase], z_recv.at[phase])
        both = start(z_list[:9], *sems, lambda t: s.at[t], r.at[me_s], lambda t: r.at[t])
        for pair_ in both:
            pair_[0].wait_send()
        del started[-9:]
        both = both + start(z_list[9:], *sems, lambda t: s.at[t], r.at[me_s], lambda t: r.at[t])
        r[me_s] = s[me_s]
        return both

    def start_c(phase, src_at, dst_at, own):
        both = start(c_list, col_send.at[phase], col_recv.at[phase], src_at, dst_at(me_p), dst_at)
        own()
        return both

    def pass_on(k, src, dst):
        go = pltpu.make_async_remote_copy(
            src_ref=src, dst_ref=dst, send_sem=twin_send.at[k], recv_sem=twin_recv.at[k],
            device_id=twin, device_id_type=MESH,
        )
        go.start()
        started.append((go, go))
        return started[-1:]

    def start_d(phase, s, r):
        both = start(d_list, depth_send.at[phase], depth_recv.at[phase], lambda t: s, r.at[me_d], lambda t: r.at[t])
        r[me_d] = s[...]
        return both

    slot = lax.broadcasted_iota(jnp.int32, (1, 1, LANE), 2) // SLOT
    chunk = lax.broadcasted_iota(jnp.int32, (1, 1, LANE), 2) % SLOT // PAD_LANES
    chunk2 = lax.broadcasted_iota(jnp.int32, (1, LANE), 1) % SLOT // PAD_LANES

    def padded_t(ref):
        pad[:, :k_block, :] = ref[...].astype(F32)
        pad[:, k_block:, :] = jnp.zeros((i_q, SLOT - k_block, ch), F32)
        return pad[...].reshape(width, ch).T

    def pack(x):
        return jnp.stack([lanes(x, v).reshape(n_z, hz, LANE) for v in range(vl)], axis=1).astype(BF16)

    fetch[0].wait()
    x_hat, inv_std = norm_rows(padded_t(pair))
    normed = x_hat.astype(BF16)
    fetch[1].wait()
    w_in_t = w_in[...].astype(F32).T.astype(BF16)
    fetch[2].wait()
    lane_id = lax.broadcasted_iota(jnp.int32, (1, width), 1)
    row_mask = jnp.zeros((1, width), F32)
    for i in range(i_q):
        here = mask[me_r * i_block + me_d * i_q + i].astype(F32)
        row_mask = jnp.where(lane_id // SLOT == i, here, row_mask)
    col_mask = jnp.zeros((1, width), F32)
    for t in range(k_block):
        here = mask[me_c * k_block + t].astype(F32)
        col_mask = jnp.where(lane_id % SLOT == t, here, col_mask)
    pair_mask = row_mask * col_mask
    parts = []
    for block in range(2):
        both = dot(w_in_t[2 * block * hid : 2 * (block + 1) * hid], normed)
        sig, val = jax.nn.sigmoid(both[:hid]), both[hid:]
        proj[2 * block] = sig
        proj[2 * block + 1] = val
        out = pair_mask * sig * val
        parts.append([lanes(out, v).reshape(n_z, hz, LANE) for v in range(vl)])
    s1[...] = jnp.stack(fold(*parts, chunk), axis=1).astype(BF16)

    pl.semaphore_wait(barrier, len(peers))
    move = start_z(0, s1, r1)
    for f in fetch[3:]:
        f.wait()
    cot_t = padded_t(cot)
    gate_val = jax.nn.sigmoid(dot(w_gate[...].astype(F32).T.astype(BF16), normed))
    w_out_t = w_out[...].astype(F32).T.astype(BF16)
    arrive(move)

    x = r1[...].astype(F32)
    a_tiles, b_tiles = unfold([x[:, j] for j in range(2 * vl - 1)], chunk)
    for v in range(vl):
        f1[v] = jnp.concatenate([a_tiles[v], b_tiles[v]], axis=1).reshape(n_z * 2 * hz, LANE)
    for h in range(hz):
        for v in range(vl):
            a0, b0, a1, b1 = (
                f1[v, pl.ds(dd * half * 2 * hz + block * hz + h, half, stride=2 * hz), :]
                for dd in range(2) for block in range(2)
            )
            at = slice(v * LANE, (v + 1) * LANE)
            s2[2 * h, :, at] = jnp.concatenate([b0, b1, a0, a1], axis=0).astype(BF16)
            s2[2 * h + 1, :, at] = jnp.concatenate([b0, b1, a1, a0], axis=0).astype(BF16)

    def own_2():
        r2[me_p] = s2[me_p]

    b_part, a_part = slice(0, 2 * half), slice(2 * half, 4 * half)
    pass_b = start(
        x_list, over_send.at[0], over_recv.at[0],
        lambda t: s2.at[t, b_part], t2.at[me_p, b_part], lambda t: t2.at[t, b_part],
    )
    move = start_c(0, lambda t: s2.at[t], lambda t: r2.at[t], own_2)
    arrive(move)
    pass_a = pass_on(1, r2.at[:, a_part], t2.at[:, a_part])
    x = r2[:, a_part, :].astype(F32)
    a_rows = to_matrix([lanes(x, v) for v in range(vl)], slot)
    a_own = jnp.concatenate([m[:half] for m in a_rows], axis=0).astype(BF16)

    def place_b(core, ref):
        x = ref[:, b_part, :].astype(F32)
        for i, m in enumerate(to_matrix([lanes(x, v) for v in range(vl)], slot)):
            for dd in range(n_dd):
                at = (dd * i_q + i) * half
                for g in range(groups):
                    bn[g, core, at : at + half, :] = lanes(m[dd * half : (dd + 1) * half], g)

    place_b(me_core, r2)
    arrive(pass_b)
    place_b(1 - me_core, t2)
    rows = []
    for core in range(2):
        for q in range(half):
            rows.append(jnp.concatenate(
                [bn[g, core, pl.ds(q, k_block, stride=half), :] for g in range(groups)], axis=-1
            ))
            rows.append(jnp.zeros((SLOT - k_block, full), F32))
    b_mat = jnp.concatenate(rows, axis=0).astype(BF16)
    tri = lax.dot_general(a_own, b_mat, (((1,), (1,)), ((), ())), preferred_element_type=F32)
    for c, x in enumerate(from_matrix(tri.reshape(i_q, half, full), slot)):
        s3[c] = x.astype(BF16)
    size3 = vl * half

    def own_3():
        r3[me_p] = s3[me_p]

    move = start_c(2, lambda t: s3.at[t], lambda t: r3.at[t], own_3)

    all_a[me_core] = jnp.concatenate(a_rows, axis=0).astype(BF16)
    arrive(pass_a)
    x = t2[:, a_part, :].astype(F32)
    all_a[1 - me_core] = jnp.concatenate(to_matrix([lanes(x, v) for v in range(vl)], slot), axis=0).astype(BF16)
    arrive(move)

    f3[...] = r3[...].astype(F32).reshape(n_c * size3, LANE)
    for dd in range(n_dd):
        for q in range(half):
            parts = [f3[pl.ds(dd * size3 + v * half + q, hz, stride=2 * size3), :] for v in range(vl)]
            s4[dd * half + q] = jnp.stack(parts, axis=0).astype(BF16)
    move = start_z(1, s4, r4)
    arrive(move)

    x = r4[...].astype(F32)
    tri_t = jnp.concatenate([x[:, v].reshape(hid, LANE) for v in range(vl)], axis=-1)
    y_hat, tri_std = norm_rows(tri_t)
    out_proj = dot(w_out_t, y_hat.astype(BF16))
    d_o = (cot_t * gate_val).astype(BF16)
    d_y = dot(w_out[...], d_o)
    s5[...] = pack(norm_back(y_hat, tri_std, d_y))
    move = start_z(2, s5, r5)

    def natural(x):
        return x.T.reshape(i_q, SLOT, ch)[:, :k_block, :].reshape(i_q * k_block, ch).astype(BF16)

    su[...] = natural(gate_val * out_proj)
    d_gate_pre = (cot_t * out_proj * gate_val * (1.0 - gate_val)).astype(BF16)
    d_gate = dot(w_gate[...], d_gate_pre)
    arrive(move)

    pitch = vl * hz
    f5[...] = r5[...].astype(F32).reshape(n_z * pitch, LANE)
    for h in range(hz):
        for v in range(vl):
            t0, t1 = (f5[pl.ds(dd * half * pitch + v * hz + h, half, stride=pitch), :] for dd in range(2))
            at = slice(v * LANE, (v + 1) * LANE)
            s6[2 * h, :, at] = jnp.concatenate([t0, t1], axis=0).astype(BF16)
            s6[2 * h + 1, :, at] = jnp.concatenate([t1, t0], axis=0).astype(BF16)

    def own_6():
        r6[me_p] = s6[me_p]

    pass_t = start(x_list, over_send.at[1], over_recv.at[1], lambda t: s6.at[t], t6.at[me_p], lambda t: t6.at[t])
    move = start_c(3, lambda t: s6.at[t], lambda t: r6.at[t], own_6)
    arrive(move)
    update_move = start_d(0, su, ru)
    x = r6[...].astype(F32)
    rows = to_matrix([lanes(x, v) for v in range(vl)], slot)
    for i, m in enumerate(rows):
        tgf[me_core, i] = m
    tg_own = jnp.concatenate([m[:half] for m in rows], axis=0).astype(BF16)
    grad_a = dot(tg_own, b_mat).reshape(i_q, half, full)
    arrive(pass_t)
    x = t6[...].astype(F32)
    for i, m in enumerate(to_matrix([lanes(x, v) for v in range(vl)], slot)):
        tgf[1 - me_core, i] = m
    mine = pl.ds(pl.multiple_of(me_core * (full // 2), full // 2), full // 2)
    tg_t = tgf[:, :, :, mine].reshape(2 * i_q * 2 * half, full // 2).T.astype(BF16)
    part_b = dot(tg_t, all_a[...].reshape(2 * i_q * 2 * half, full))
    for g in range(groups):
        gf[g] = lanes(part_b, g)
    rows = []
    for i in range(i_q):
        rows.append(grad_a[i])
        rows.append(jnp.concatenate(
            [gf[g, pl.ds(me_dd * i_q + i, half, stride=SLOT), :] for g in range(groups)], axis=-1
        ))
    both = jnp.concatenate(rows, axis=0).reshape(i_q, 2 * half, full)
    for c, x in enumerate(from_matrix(both, slot)):
        for v in range(vl):
            s8[c, :, v * LANE : (v + 1) * LANE] = x[v].astype(BF16)

    def own_8():
        r8[me_p] = s8[me_p]

    move = start_c(4, lambda t: s8.at[t], lambda t: r8.at[t], own_8)
    arrive(move)
    x = r8[...].astype(F32)
    for v in range(vl):
        f8[v] = lanes(x, v).reshape(n_c * 2 * half, LANE)
    for dd in range(n_dd):
        for q in range(half):
            a_tiles, b_tiles = (
                [f8[v, pl.ds((dd * 2 + block) * half + q, hz, stride=4 * half), :] for v in range(vl)]
                for block in range(2)
            )
            s9[dd * half + q] = jnp.stack(fold(a_tiles, b_tiles, chunk2), axis=0).astype(BF16)
    move = start_z(3, s9, r9)
    arrive(move)

    d_normed = d_gate
    x = r9[...].astype(F32)
    grads = unfold([x[:, j] for j in range(2 * vl - 1)], chunk)
    for block in range(2):
        grad = jnp.concatenate([g.reshape(hid, LANE) for g in grads[block]], axis=-1) * pair_mask
        sig, val = proj[2 * block], proj[2 * block + 1]
        d_pre = (grad * val * sig * (1.0 - sig)).astype(BF16)
        d_val = (grad * sig).astype(BF16)
        d_normed = d_normed + dot(w_in[:, 2 * block * hid : (2 * block + 1) * hid], d_pre)
        d_normed = d_normed + dot(w_in[:, (2 * block + 1) * hid : (2 * block + 2) * hid], d_val)
    sg[...] = natural(norm_back(x_hat, inv_std, d_normed))
    move = start_d(1, sg, rg)
    arrive(update_move)
    for d in range(n_d):
        update_out[d * i_q : (d + 1) * i_q] = ru[d].astype(F32).reshape(i_q, k_block, ch).astype(BF16)
    arrive(move)
    for d in range(n_d):
        grad_out[d * i_q : (d + 1) * i_q] = rg[d].astype(F32).reshape(i_q, k_block, ch).astype(BF16)
    for go, _ in started:
        go.wait_send()


def shards(sizes, pair, cotangent, w_in, w_gate, w_out, residue_mask):
    n_d, n_r, n_c = sizes
    n_x = 4 if n_c == 16 else 2
    i_block, k_block, ch = pair.shape
    hid = w_out.shape[0]
    i_q = i_block // n_d
    width = i_q * SLOT
    vl = width // LANE
    n_z = (n_r // 2) * n_d
    half = n_r
    hz = hid // n_z
    full = n_c * SLOT
    groups = max(full // LANE, 1)
    pitch = vl * hz
    vm = pltpu.VMEM
    operands = [
        pltpu.with_memory_space_constraint(v, pltpu.HBM)
        for v in (residue_mask, pair, cotangent, w_in, w_gate, w_out)
    ]
    scratch = [
        pltpu.SMEM(residue_mask.shape, jnp.int32),
        vm((i_q, k_block, ch), BF16),
        vm((i_q, k_block, ch), BF16),
        vm(w_in.shape, BF16),
        vm(w_gate.shape, BF16),
        vm(w_out.shape, BF16),
        pltpu.SemaphoreType.DMA((6,)),
        vm((i_q, SLOT, ch), F32),
        vm((4, hid, width), F32),
        vm((n_z, 2 * vl - 1, hz, LANE), BF16),
        vm((n_z, 2 * vl - 1, hz, LANE), BF16),
        vm((vl, n_z * 2 * hz, LANE), F32),
        vm((n_c, 4 * half, width), BF16),
        vm((n_c, 4 * half, width), BF16),
        vm((n_c, 4 * half, width), BF16),
        vm((groups, 2, k_block * half, LANE), F32),
        vm((2, i_q * 2 * half, full), BF16),
        vm((n_c, vl, half, LANE), BF16),
        vm((n_c, vl, half, LANE), BF16),
        vm((n_c * vl * half, LANE), F32),
        vm((n_z, vl, hz, LANE), BF16),
        vm((n_z, vl, hz, LANE), BF16),
        vm((n_z, vl, hz, LANE), BF16),
        vm((n_z, vl, hz, LANE), BF16),
        vm((n_z * pitch, LANE), F32),
        vm((n_c, 2 * half, width), BF16),
        vm((n_c, 2 * half, width), BF16),
        vm((n_c, 2 * half, width), BF16),
        vm((2, i_q, 2 * half, full), F32),
        vm((groups, full // 2, LANE), F32),
        vm((n_c, 2 * half, width), BF16),
        vm((n_c, 2 * half, width), BF16),
        vm((vl, n_c * 2 * half, LANE), F32),
        vm((n_z, 2 * vl - 1, hz, LANE), BF16),
        vm((n_z, 2 * vl - 1, hz, LANE), BF16),
        vm((i_q * k_block, ch), BF16),
        vm((n_d, i_q * k_block, ch), BF16),
        vm((i_q * k_block, ch), BF16),
        vm((n_d, i_q * k_block, ch), BF16),
    ]
    for phases, size in ((4, n_z), (5, n_c), (2, n_d)):
        scratch += [pltpu.SemaphoreType.DMA((phases, size))] * 2
    scratch += [pltpu.SemaphoreType.DMA((2, n_c))] * 2
    scratch += [pltpu.SemaphoreType.DMA((3,))] * 2
    whole = pl.BlockSpec(memory_space=pltpu.VMEM)
    return pl.pallas_call(
        functools.partial(kernel, (n_d, n_r, n_c, n_x, i_block, k_block, ch, hid)),
        out_shape=(jax.ShapeDtypeStruct(pair.shape, BF16),) * 2,
        in_specs=[pl.BlockSpec(memory_space=pl.ANY)] * 6,
        out_specs=(whole, whole),
        scratch_shapes=scratch,
        compiler_params=pltpu.CompilerParams(
            collective_id=0, has_side_effects=True, vmem_limit_bytes=40 * 1024 * 1024
        ),
    )(*operands)


def solution(mesh):
    in_specs = (P("row", "col", None), P("row", "col", None), P(), P(), P(), P())
    out_specs = (P("row", "col", None), P("row", "col", None))
    sizes = (mesh.shape["depth"], mesh.shape["row"], mesh.shape["col"])
    return jax.shard_map(
        functools.partial(shards, sizes), mesh=mesh, in_specs=in_specs, out_specs=out_specs, check_vma=False
    )
```

```python
import functools

import jax
import jax.numpy as jnp
from jax import lax
from jax.experimental import pallas as pl
from jax.experimental.pallas import tpu as pltpu
from jax.sharding import PartitionSpec as P

MESH = pl.DeviceIdType.MESH
F32 = jnp.float32
BF16 = jnp.bfloat16
SLOT = 32
LANE = 128
PER = LANE // SLOT
PAD_LANES = 8


def dot(left, right):
    return jnp.dot(left, right, preferred_element_type=F32)


def norm_rows(values):
    average = jnp.mean(values, axis=0, keepdims=True)
    centered = values - average
    variance = jnp.mean(centered * centered, axis=0, keepdims=True)
    inv_std = lax.rsqrt(variance + 1e-05)
    return (centered * inv_std, inv_std)


def norm_back(x_hat, inv_std, upstream):
    first = jnp.mean(upstream, axis=0, keepdims=True)
    second = jnp.mean(upstream * x_hat, axis=0, keepdims=True)
    return inv_std * (upstream - first - x_hat * second)


def lanes(x, v):
    return x[..., v * LANE : (v + 1) * LANE]


def to_matrix(tiles, slot):
    out = []
    for x in tiles:
        groups, rows = x.shape[0] // PER, x.shape[1]
        x = x.reshape(groups, PER, rows, LANE)
        for s in range(PER):
            acc = None
            for c in range(PER):
                y = x[:, c]
                if c != s:
                    y = pltpu.roll(y, (SLOT * (c - s)) % LANE, 2)
                acc = y if acc is None else jnp.where(slot == c, y, acc)
            out.append(jnp.concatenate([acc[g] for g in range(groups)], axis=-1))
    return out


def fold(a, b, chunk):
    last, per_slot = b[-1], SLOT // PAD_LANES
    out = []
    for j, tile in enumerate(a):
        moved = pltpu.roll(last, PAD_LANES * (per_slot - 1 - j), last.ndim - 1)
        out.append(jnp.where(chunk == per_slot - 1, moved, tile))
    return out + b[:-1]


def unfold(tiles, chunk):
    per_slot = SLOT // PAD_LANES
    last = jnp.zeros_like(tiles[0])
    a = []
    for j, tile in enumerate(tiles[: per_slot - 1]):
        moved = pltpu.roll(tile, LANE - PAD_LANES * (per_slot - 1 - j), tile.ndim - 1)
        last = jnp.where(chunk == j, moved, last)
        a.append(jnp.where(chunk == per_slot - 1, 0.0, tile))
    return a, tiles[per_slot - 1 :] + [last]


def from_matrix(matrix, slot):
    count, rows, width = matrix.shape
    x = matrix.reshape(count // PER, PER, rows, width)
    out = []
    for g in range(width // LANE):
        part = lanes(x, g)
        for c in range(PER):
            acc = None
            for s in range(PER):
                y = part[:, s]
                if c != s:
                    y = pltpu.roll(y, (SLOT * (s - c)) % LANE, 2)
                acc = y if acc is None else jnp.where(slot == s, y, acc)
            out.append(acc)
    return out


def kernel(
    dims,
    mask_hbm, pair_hbm, cot_hbm, w_in_hbm, w_gate_hbm, w_out_hbm,
    update_out, grad_out,
    mask, pair, cot, w_in, w_gate, w_out, in_sem,
    pad, proj, s1, r1, f1, s2, r2, t2, bn, all_a, s3, r3, f3, s4, r4, s5, r5, f5, s6, r6, t6, tgf,
    gf, s8, r8, f8, s9, r9, su, ru, sg, rg,
    z_send, z_recv, col_send, col_recv, depth_send, depth_recv, over_send, over_recv, twin_send, twin_recv,
):
    n_d, n_r, n_c, n_x, i_block, k_block, ch, hid = dims
    n_zh, n_dd, n_y = n_r // 2, n_d // 2, n_c // n_x
    n_z = n_zh * n_d
    hz = hid // n_z
    i_q = i_block // n_d
    width = i_q * SLOT
    vl = width // LANE
    half = 2 * n_zh
    full = n_c * SLOT
    groups = full // LANE
    me_d, me_r, me_c = lax.axis_index("depth"), lax.axis_index("row"), lax.axis_index("col")
    me_zh, me_core = me_r // 2, me_r % 2

    def z_slot(zh, d):
        return (d % n_dd) * half + (d // n_dd) * n_zh + zh

    def c_slot(c):
        return ((c // 2) % 2) * half + (c % 2) * n_zh + c // 4

    me_s, me_p = z_slot(me_zh, me_d), c_slot(me_c)
    me_dd = me_p % 2

    def z_peer(o):
        z = lax.rem(me_zh * n_d + me_d + o + n_z, n_z)
        zh, d = z // n_d, z % n_d
        return {"row": zh * 2 + me_core, "depth": d}, z_slot(zh, d)

    def c_peer(ox, oy):
        x = lax.rem(me_c // n_y + ox + n_x, n_x)
        y = lax.rem(me_c % n_y + oy + n_y, n_y)
        c = x * n_y + y
        return {"col": c}, c_slot(c)

    def d_peer(o):
        d = lax.rem(me_d + o + n_d, n_d)
        return {"depth": d}, d

    z_offsets = sorted(range(1, n_z), key=lambda o: -min(o, n_z - o))
    c_offsets = sorted(
        [(x, y) for x in range(n_x) for y in range(n_y)],
        key=lambda o: -(min(o[0], n_x - o[0]) + min(o[1], n_y - o[1])),
    )
    d_offsets = list(range(1, n_d))

    z_list = [z_peer(o) + (z_peer(-o)[1], k) for k, o in enumerate(z_offsets)]
    d_list = [d_peer(o) + (d_peer(-o)[1], k) for k, o in enumerate(d_offsets)]
    c_list = [
        c_peer(ox, oy) + (c_peer(-ox, -oy)[1], k) for k, (ox, oy) in enumerate(c_offsets) if (ox, oy) != (0, 0)
    ]
    x_list = []
    for k, (ox, oy) in enumerate(c_offsets):
        to, slot_to = c_peer(ox, oy)
        x_list.append(({**to, "row": me_zh * 2 + 1 - me_core}, slot_to, c_peer(-ox, -oy)[1], k))
    twin = {"row": me_zh * 2 + 1 - me_core}

    barrier = pltpu.get_barrier_semaphore()
    peers = [to for to, _, _, _ in z_list + c_list + x_list]
    for to in peers:
        pl.semaphore_signal(barrier, inc=1, device_id=to, device_id_type=MESH)

    own_rows = pl.ds(me_d * i_q, i_q)
    fetch = [
        pltpu.make_async_copy(a, b, in_sem.at[k])
        for k, (a, b) in enumerate([
            (pair_hbm.at[own_rows], pair), (w_in_hbm, w_in), (mask_hbm, mask),
            (cot_hbm.at[own_rows], cot), (w_gate_hbm, w_gate), (w_out_hbm, w_out),
        ])
    ]
    for f in fetch:
        f.start()

    started = []

    def start(peer_list, send, recv, src_at, dst_mine, dst_from):
        both = []
        for to, slot_to, slot_from, k in peer_list:
            go = pltpu.make_async_remote_copy(
                src_ref=src_at(slot_to), dst_ref=dst_mine, send_sem=send.at[k], recv_sem=recv.at[k],
                device_id=to, device_id_type=MESH,
            )
            come = pltpu.make_async_remote_copy(
                src_ref=src_at(slot_to), dst_ref=dst_from(slot_from), send_sem=send.at[k], recv_sem=recv.at[k],
                device_id=to, device_id_type=MESH,
            )
            go.start()
            both.append((go, come))
        started.extend(both)
        return both

    def arrive(both):
        for _, come in both:
            come.wait_recv()

    def start_z(phase, s, r):
        sems = (z_send.at[phase], z_recv.at[phase])
        both = start(z_list[:9], *sems, lambda t: s.at[t], r.at[me_s], lambda t: r.at[t])
        for pair_ in both:
            pair_[0].wait_send()
        del started[-9:]
        both = both + start(z_list[9:], *sems, lambda t: s.at[t], r.at[me_s], lambda t: r.at[t])
        r[me_s] = s[me_s]
        return both

    def start_c(phase, src_at, dst_at, own):
        both = start(c_list, col_send.at[phase], col_recv.at[phase], src_at, dst_at(me_p), dst_at)
        own()
        return both

    def pass_on(k, src, dst):
        go = pltpu.make_async_remote_copy(
            src_ref=src, dst_ref=dst, send_sem=twin_send.at[k], recv_sem=twin_recv.at[k],
            device_id=twin, device_id_type=MESH,
        )
        go.start()
        started.append((go, go))
        return started[-1:]

    def start_d(phase, s, r):
        both = start(d_list, depth_send.at[phase], depth_recv.at[phase], lambda t: s, r.at[me_d], lambda t: r.at[t])
        r[me_d] = s[...]
        return both

    slot = lax.broadcasted_iota(jnp.int32, (1, 1, LANE), 2) // SLOT
    chunk = lax.broadcasted_iota(jnp.int32, (1, 1, LANE), 2) % SLOT // PAD_LANES
    chunk2 = lax.broadcasted_iota(jnp.int32, (1, LANE), 1) % SLOT // PAD_LANES

    def padded_t(ref):
        pad[:, :k_block, :] = ref[...].astype(F32)
        pad[:, k_block:, :] = jnp.zeros((i_q, SLOT - k_block, ch), F32)
        return pad[...].reshape(width, ch).T

    def pack(x):
        return jnp.stack([lanes(x, v).reshape(n_z, hz, LANE) for v in range(vl)], axis=1).astype(BF16)

    fetch[0].wait()
    x_hat, inv_std = norm_rows(padded_t(pair))
    normed = x_hat.astype(BF16)
    fetch[1].wait()
    w_in_t = w_in[...].astype(F32).T.astype(BF16)
    fetch[2].wait()
    lane_id = lax.broadcasted_iota(jnp.int32, (1, width), 1)
    row_mask = jnp.zeros((1, width), F32)
    for i in range(i_q):
        here = mask[me_r * i_block + me_d * i_q + i].astype(F32)
        row_mask = jnp.where(lane_id // SLOT == i, here, row_mask)
    col_mask = jnp.zeros((1, width), F32)
    for t in range(k_block):
        here = mask[me_c * k_block + t].astype(F32)
        col_mask = jnp.where(lane_id % SLOT == t, here, col_mask)
    pair_mask = row_mask * col_mask
    parts = []
    for block in range(2):
        both = dot(w_in_t[2 * block * hid : 2 * (block + 1) * hid], normed)
        sig, val = jax.nn.sigmoid(both[:hid]), both[hid:]
        proj[2 * block] = sig
        proj[2 * block + 1] = val
        out = pair_mask * sig * val
        parts.append([lanes(out, v).reshape(n_z, hz, LANE) for v in range(vl)])
    s1[...] = jnp.stack(fold(*parts, chunk), axis=1).astype(BF16)

    pl.semaphore_wait(barrier, len(peers))
    move = start_z(0, s1, r1)
    for f in fetch[3:]:
        f.wait()
    cot_t = padded_t(cot)
    gate_val = jax.nn.sigmoid(dot(w_gate[...].astype(F32).T.astype(BF16), normed))
    w_out_t = w_out[...].astype(F32).T.astype(BF16)
    arrive(move)

    x = r1[...].astype(F32)
    a_tiles, b_tiles = unfold([x[:, j] for j in range(2 * vl - 1)], chunk)
    for v in range(vl):
        f1[v] = jnp.concatenate([a_tiles[v], b_tiles[v]], axis=1).reshape(n_z * 2 * hz, LANE)
    for h in range(hz):
        for v in range(vl):
            a0, b0, a1, b1 = (
                f1[v, pl.ds(dd * half * 2 * hz + block * hz + h, half, stride=2 * hz), :]
                for dd in range(2) for block in range(2)
            )
            at = slice(v * LANE, (v + 1) * LANE)
            s2[2 * h, :, at] = jnp.concatenate([b0, b1, a0, a1], axis=0).astype(BF16)
            s2[2 * h + 1, :, at] = jnp.concatenate([b0, b1, a1, a0], axis=0).astype(BF16)

    def own_2():
        r2[me_p] = s2[me_p]

    b_part, a_part = slice(0, 2 * half), slice(2 * half, 4 * half)
    pass_b = start(
        x_list, over_send.at[0], over_recv.at[0],
        lambda t: s2.at[t, b_part], t2.at[me_p, b_part], lambda t: t2.at[t, b_part],
    )
    move = start_c(0, lambda t: s2.at[t], lambda t: r2.at[t], own_2)
    arrive(move)
    pass_a = pass_on(1, r2.at[:, a_part], t2.at[:, a_part])
    x = r2[:, a_part, :].astype(F32)
    a_rows = to_matrix([lanes(x, v) for v in range(vl)], slot)
    a_own = jnp.concatenate([m[:half] for m in a_rows], axis=0).astype(BF16)

    def place_b(core, ref):
        x = ref[:, b_part, :].astype(F32)
        for i, m in enumerate(to_matrix([lanes(x, v) for v in range(vl)], slot)):
            for dd in range(n_dd):
                at = (dd * i_q + i) * half
                for g in range(groups):
                    bn[g, core, at : at + half, :] = lanes(m[dd * half : (dd + 1) * half], g)

    place_b(me_core, r2)
    arrive(pass_b)
    place_b(1 - me_core, t2)
    rows = []
    for core in range(2):
        for q in range(half):
            rows.append(jnp.concatenate(
                [bn[g, core, pl.ds(q, k_block, stride=half), :] for g in range(groups)], axis=-1
            ))
            rows.append(jnp.zeros((SLOT - k_block, full), F32))
    b_mat = jnp.concatenate(rows, axis=0).astype(BF16)
    tri = lax.dot_general(a_own, b_mat, (((1,), (1,)), ((), ())), preferred_element_type=F32)
    for c, x in enumerate(from_matrix(tri.reshape(i_q, half, full), slot)):
        s3[c] = x.astype(BF16)
    size3 = vl * half

    def own_3():
        r3[me_p] = s3[me_p]

    move = start_c(2, lambda t: s3.at[t], lambda t: r3.at[t], own_3)

    all_a[me_core] = jnp.concatenate(a_rows, axis=0).astype(BF16)
    arrive(pass_a)
    x = t2[:, a_part, :].astype(F32)
    all_a[1 - me_core] = jnp.concatenate(to_matrix([lanes(x, v) for v in range(vl)], slot), axis=0).astype(BF16)
    arrive(move)

    f3[...] = r3[...].astype(F32).reshape(n_c * size3, LANE)
    for dd in range(n_dd):
        for q in range(half):
            parts = [f3[pl.ds(dd * size3 + v * half + q, hz, stride=2 * size3), :] for v in range(vl)]
            s4[dd * half + q] = jnp.stack(parts, axis=0).astype(BF16)
    move = start_z(1, s4, r4)
    arrive(move)

    x = r4[...].astype(F32)
    tri_t = jnp.concatenate([x[:, v].reshape(hid, LANE) for v in range(vl)], axis=-1)
    y_hat, tri_std = norm_rows(tri_t)
    out_proj = dot(w_out_t, y_hat.astype(BF16))
    d_o = (cot_t * gate_val).astype(BF16)
    d_y = dot(w_out[...], d_o)
    s5[...] = pack(norm_back(y_hat, tri_std, d_y))
    move = start_z(2, s5, r5)

    def natural(x):
        return x.T.reshape(i_q, SLOT, ch)[:, :k_block, :].reshape(i_q * k_block, ch).astype(BF16)

    su[...] = natural(gate_val * out_proj)
    d_gate_pre = (cot_t * out_proj * gate_val * (1.0 - gate_val)).astype(BF16)
    d_gate = dot(w_gate[...], d_gate_pre)
    arrive(move)

    pitch = vl * hz
    f5[...] = r5[...].astype(F32).reshape(n_z * pitch, LANE)
    for h in range(hz):
        for v in range(vl):
            t0, t1 = (f5[pl.ds(dd * half * pitch + v * hz + h, half, stride=pitch), :] for dd in range(2))
            at = slice(v * LANE, (v + 1) * LANE)
            s6[2 * h, :, at] = jnp.concatenate([t0, t1], axis=0).astype(BF16)
            s6[2 * h + 1, :, at] = jnp.concatenate([t1, t0], axis=0).astype(BF16)

    def own_6():
        r6[me_p] = s6[me_p]

    pass_t = start(x_list, over_send.at[1], over_recv.at[1], lambda t: s6.at[t], t6.at[me_p], lambda t: t6.at[t])
    move = start_c(3, lambda t: s6.at[t], lambda t: r6.at[t], own_6)
    arrive(move)
    update_move = start_d(0, su, ru)
    x = r6[...].astype(F32)
    rows = to_matrix([lanes(x, v) for v in range(vl)], slot)
    for i, m in enumerate(rows):
        tgf[me_core, i] = m
    tg_own = jnp.concatenate([m[:half] for m in rows], axis=0).astype(BF16)
    grad_a = dot(tg_own, b_mat).reshape(i_q, half, full)
    arrive(pass_t)
    x = t6[...].astype(F32)
    for i, m in enumerate(to_matrix([lanes(x, v) for v in range(vl)], slot)):
        tgf[1 - me_core, i] = m
    mine = pl.ds(pl.multiple_of(me_core * (full // 2), full // 2), full // 2)
    tg_t = tgf[:, :, :, mine].reshape(2 * i_q * 2 * half, full // 2).T.astype(BF16)
    part_b = dot(tg_t, all_a[...].reshape(2 * i_q * 2 * half, full))
    for g in range(groups):
        gf[g, : full // 2] = lanes(part_b, g)
    rows = []
    for i in range(i_q):
        rows.append(grad_a[i])
        rows.append(jnp.concatenate(
            [gf[g, pl.ds(me_dd * i_q + i, half, stride=SLOT), :] for g in range(groups)], axis=-1
        ))
    both = jnp.concatenate(rows, axis=0).reshape(i_q, 2 * half, full)
    for c, x in enumerate(from_matrix(both, slot)):
        for v in range(vl):
            s8[c, :, v * LANE : (v + 1) * LANE] = x[v].astype(BF16)

    def own_8():
        r8[me_p] = s8[me_p]

    move = start_c(4, lambda t: s8.at[t], lambda t: r8.at[t], own_8)
    arrive(move)
    x = r8[...].astype(F32)
    for v in range(vl):
        f8[v] = lanes(x, v).reshape(n_c * 2 * half, LANE)
    for dd in range(n_dd):
        for q in range(half):
            a_tiles, b_tiles = (
                [f8[v, pl.ds((dd * 2 + block) * half + q, hz, stride=4 * half), :] for v in range(vl)]
                for block in range(2)
            )
            s9[dd * half + q] = jnp.stack(fold(a_tiles, b_tiles, chunk2), axis=0).astype(BF16)
    move = start_z(3, s9, r9)
    arrive(move)

    d_normed = d_gate
    x = r9[...].astype(F32)
    grads = unfold([x[:, j] for j in range(2 * vl - 1)], chunk)
    for block in range(2):
        grad = jnp.concatenate([g.reshape(hid, LANE) for g in grads[block]], axis=-1) * pair_mask
        sig, val = proj[2 * block], proj[2 * block + 1]
        d_pre = (grad * val * sig * (1.0 - sig)).astype(BF16)
        d_val = (grad * sig).astype(BF16)
        d_normed = d_normed + dot(w_in[:, 2 * block * hid : (2 * block + 1) * hid], d_pre)
        d_normed = d_normed + dot(w_in[:, (2 * block + 1) * hid : (2 * block + 2) * hid], d_val)
    sg[...] = natural(norm_back(x_hat, inv_std, d_normed))
    move = start_d(1, sg, rg)
    arrive(update_move)
    for d in range(n_d):
        update_out[d * i_q : (d + 1) * i_q] = ru[d].astype(F32).reshape(i_q, k_block, ch).astype(BF16)
    arrive(move)
    for d in range(n_d):
        grad_out[d * i_q : (d + 1) * i_q] = rg[d].astype(F32).reshape(i_q, k_block, ch).astype(BF16)
    for go, _ in started:
        go.wait_send()


def shards(sizes, pair, cotangent, w_in, w_gate, w_out, residue_mask):
    n_d, n_r, n_c = sizes
    n_x = 4 if n_c == 16 else 2
    i_block, k_block, ch = pair.shape
    hid = w_out.shape[0]
    i_q = i_block // n_d
    width = i_q * SLOT
    vl = width // LANE
    n_z = (n_r // 2) * n_d
    half = n_r
    hz = hid // n_z
    full = n_c * SLOT
    groups = max(full // LANE, 1)
    pitch = vl * hz
    vm = pltpu.VMEM
    operands = [
        pltpu.with_memory_space_constraint(v, pltpu.HBM)
        for v in (residue_mask, pair, cotangent, w_in, w_gate, w_out)
    ]
    scratch = [
        pltpu.SMEM(residue_mask.shape, jnp.int32),
        vm((i_q, k_block, ch), BF16),
        vm((i_q, k_block, ch), BF16),
        vm(w_in.shape, BF16),
        vm(w_gate.shape, BF16),
        vm(w_out.shape, BF16),
        pltpu.SemaphoreType.DMA((6,)),
        vm((i_q, SLOT, ch), F32),
        vm((4, hid, width), F32),
        vm((n_z, 2 * vl - 1, hz, LANE), BF16),
        vm((n_z, 2 * vl - 1, hz, LANE), BF16),
        vm((vl, n_z * 2 * hz, LANE), F32),
        vm((n_c, 4 * half, width), BF16),
        vm((n_c, 4 * half, width), BF16),
        vm((n_c, 4 * half, width), BF16),
        vm((groups, 2, k_block * half, LANE), F32),
        vm((2, i_q * 2 * half, full), BF16),
        vm((n_c, vl, half, LANE), BF16),
        vm((n_c, vl, half, LANE), BF16),
        vm((n_c * vl * half, LANE), F32),
        vm((n_z, vl, hz, LANE), BF16),
        vm((n_z, vl, hz, LANE), BF16),
        vm((n_z, vl, hz, LANE), BF16),
        vm((n_z, vl, hz, LANE), BF16),
        vm((n_z * pitch, LANE), F32),
        vm((n_c, 2 * half, width), BF16),
        vm((n_c, 2 * half, width), BF16),
        vm((n_c, 2 * half, width), BF16),
        vm((2, i_q, 2 * half, full), F32),
        vm((groups, full // 2 + SLOT, LANE), F32),
        vm((n_c, 2 * half, width), BF16),
        vm((n_c, 2 * half, width), BF16),
        vm((vl, n_c * 2 * half, LANE), F32),
        vm((n_z, 2 * vl - 1, hz, LANE), BF16),
        vm((n_z, 2 * vl - 1, hz, LANE), BF16),
        vm((i_q * k_block, ch), BF16),
        vm((n_d, i_q * k_block, ch), BF16),
        vm((i_q * k_block, ch), BF16),
        vm((n_d, i_q * k_block, ch), BF16),
    ]
    for phases, size in ((4, n_z), (5, n_c), (2, n_d)):
        scratch += [pltpu.SemaphoreType.DMA((phases, size))] * 2
    scratch += [pltpu.SemaphoreType.DMA((2, n_c))] * 2
    scratch += [pltpu.SemaphoreType.DMA((3,))] * 2
    whole = pl.BlockSpec(memory_space=pltpu.VMEM)
    return pl.pallas_call(
        functools.partial(kernel, (n_d, n_r, n_c, n_x, i_block, k_block, ch, hid)),
        out_shape=(jax.ShapeDtypeStruct(pair.shape, BF16),) * 2,
        in_specs=[pl.BlockSpec(memory_space=pl.ANY)] * 6,
        out_specs=(whole, whole),
        scratch_shapes=scratch,
        compiler_params=pltpu.CompilerParams(
            collective_id=0, has_side_effects=True, vmem_limit_bytes=40 * 1024 * 1024
        ),
    )(*operands)


def solution(mesh):
    in_specs = (P("row", "col", None), P("row", "col", None), P(), P(), P(), P())
    out_specs = (P("row", "col", None), P("row", "col", None))
    sizes = (mesh.shape["depth"], mesh.shape["row"], mesh.shape["col"])
    return jax.shard_map(
        functools.partial(shards, sizes), mesh=mesh, in_specs=in_specs, out_specs=out_specs, check_vma=False
    )
```
